256 devices in a mesh: batch: 16 (over y_lo, x, core), patch: 8 (over z), cfg: 2 (over y_hi).
Axes of the slice: x: 4, y: 4 (y_hi: 2, y_lo: 2; y = y_hi * 2 + y_lo), z: 8, core: 2. Of those that a mesh axis runs over, the one named last changes fastest.
Arguments:
- latent: float32 [128, 128, 640], P(('batch', 'patch')), parts along dimension 0, may hold values from -80 to 80
- stale_conv: bfloat16 [2, 128, 128, 640], P('cfg', ('batch', 'patch')), parts along dimension 1, may hold values from -6 to 6
- stale_attn: bfloat16 [2, 128, 128, 640], P('cfg', ('batch', 'patch')), parts along dimension 1, may hold values from -6 to 6
- cond_embed: float32 [32, 640], P(('batch', 'cfg')), parts along dimension 0, may hold values from -3 to 3
- timesteps: int32 [3], replicated, may hold values from 579 to 699, as said below
- gn_gain: float32 [640], replicated, may hold values from 0.25 to 1.75
- ln_gain: float32 [640], replicated, may hold values from 0.25 to 1.75
- time_scale: float32 [640], replicated, may hold values from -4 to 4
- conv_weight: bfloat16 [3, 3, 640, 640], replicated, may hold values from -0.078125 to 0.078125
- q_weight: bfloat16 [640, 640], replicated, may hold values from -1 to 1
- kv_weight: bfloat16 [640, 1280], replicated, may hold values from -1 to 1
- out_weight: bfloat16 [640, 640], replicated, may hold values from -0.25 to 0.25
Outputs:
- final_latent: float32 [128, 128, 640], P(('batch', 'patch')), parts along dimension 0
- final_guided: float32 [128, 128, 640], P(('batch', 'patch')), parts along dimension 0
The draws below stay inside these ranges and needn't reach their ends.
There are 16 independent parts, one for each index of `batch`. The reference program is written for one: setup_inputs(seed, part) draws one part's arguments, and reference() takes and returns one part's arrays. A program takes and returns all parts, laid end to end along the dimension named above; an argument that names none is the same for every part. Nothing has to cross between parts.
Inputs may be any that keep to these rules, and one draw needn't show every extreme that they name: `timesteps`: strictly falling; the first entry is 699 and the last is 579.
All inputs are finite; a program needn't handle non-finite values.
Results may differ from the reference program's by a relative error of at most 0.033.
Values may be sent and summed in bfloat16 or wider, within the bound.
No kernel may reach another device: no remote copies, remote signals or barrier semaphores. Data moves between devices by JAX's collectives and lax.ppermute only.
A program may use at most 128 MiB of HBM per device.

```python
import math
import jax
import jax.numpy as jnp
from jax import lax

C = 640
HEADS = 10
GROUPS = 32
HEAD_DIM = 64
COLS = 128
ROWS_DEV = 1
STEPS = 2
ROWS = 8


def draw_latent(key, part):
    key = jax.random.fold_in(key, 1)
    keys = jax.random.split(key, 4)
    trend = math.log(30.0) * jnp.arange(ROWS, dtype=jnp.float32) / (ROWS - 1)
    row_part = jax.random.uniform(keys[0], (ROWS,), jnp.float32, 0.0, math.log(3.0))
    col_part = jax.random.uniform(keys[1], (COLS,), jnp.float32, 0.0, math.log(2.0))
    chan_part = jax.random.uniform(keys[2], (C,), jnp.float32, 0.0, math.log(2.0))
    scale = 0.002 * jnp.exp((trend + row_part)[:, None, None] + col_part[None, :, None] + chan_part[None, None, :])
    base = jax.random.truncated_normal(keys[3], -4.0, 4.0, (ROWS, COLS, C), jnp.float32) + 1.0
    return (base * scale).astype(jnp.float32)


def draw_timesteps(key, part):
    key = jax.random.fold_in(key, 2)
    gaps = jax.random.randint(key, (STEPS,), 20, 41, dtype=jnp.int32)
    first = jnp.full((1,), 699, jnp.int32)
    middle = 699 - jnp.cumsum(gaps)[:STEPS - 1]
    last = jnp.full((1,), 699 - 60 * STEPS, jnp.int32)
    return jnp.concatenate([first, middle.astype(jnp.int32), last]).astype(jnp.int32)


def shared_signs(key):
    chan_key, head_key = jax.random.split(key)
    chan = jnp.where(jax.random.bernoulli(chan_key, 0.5, (C,)), 1.0, -1.0).astype(jnp.float32)
    head = jnp.where(jax.random.bernoulli(head_key, 0.5, (C,)), 1.0, -1.0).astype(jnp.float32)
    return (chan, head)


def draw_q_weight(key, part):
    chan, head = shared_signs(key)
    key = jax.random.fold_in(key, 3)
    keys = jax.random.split(key, 2)
    factor = jax.random.uniform(keys[0], (HEADS,), jnp.float32, 0.5, 1.0)
    head_scale = jnp.repeat(factor, C // HEADS)
    base = jax.random.truncated_normal(keys[1], -4.0, 4.0, (C, C), jnp.float32)
    strength = 1.5
    planted = strength * chan[:, None] * (head * head_scale)[None, :]
    return ((base + planted) * C ** (-0.5)).astype(jnp.bfloat16)


def draw_kv_weight(key, part):
    chan, head = shared_signs(key)
    key = jax.random.fold_in(key, 4)
    base = jax.random.truncated_normal(key, -4.0, 4.0, (C, 2 * C), jnp.float32)
    strength = 0.4
    planted = jnp.concatenate([strength * chan[:, None] * head[None, :], jnp.zeros((C, C), jnp.float32)], axis=1)
    return ((base + planted) * C ** (-0.5)).astype(jnp.bfloat16)


def shard_levels(own_key, shape, pieces, smallest, high):
    def one(dim, shards_of):
        steps = jax.random.uniform(jax.random.fold_in(jax.random.fold_in(own_key, 6), dim), (shards_of,), jnp.float32, smallest / len(pieces), high / len(pieces))
        return jnp.repeat(jnp.exp(steps), shape[dim] // shards_of).reshape((-1,) + (1,) * (len(shape) - dim - 1))

    loudness = one(*pieces[0])
    for cut in pieces[1:]:
        loudness = loudness * one(*cut)
    return loudness


def scatter_about(stream_key, extent, scale, most, pieces=(), held_as=jnp.bfloat16):
    level = shard_levels(stream_key, extent, pieces, -0.22, 0.18) if pieces else 1.0
    entries = jax.random.normal(stream_key, extent, jnp.float32) * scale * level
    return jnp.minimum(jnp.maximum(entries, -most), most).astype(held_as)


def setup_inputs(seed: int = 0, part: int = 0) -> dict:
    splits = jax.random.split(jax.random.key(seed), 13)
    own_keys = jax.random.split(jax.random.fold_in(splits[12], part), 13)
    return {
        "latent": draw_latent(jax.random.fold_in(jax.random.fold_in(splits[12], part), 71), part),
        "stale_conv": scatter_about(own_keys[1], (2, ROWS, COLS, C), 1.0, 6.0, ((0, 2), (1, 8))),
        "stale_attn": scatter_about(own_keys[2], (2, ROWS, COLS, C), 1.0, 6.0, ((0, 2), (1, 8))),
        "cond_embed": scatter_about(own_keys[3], (2, C), 0.5, 3.0, ((0, 2),), jnp.float32),
        "timesteps": draw_timesteps(jax.random.fold_in(splits[12], 71), part),
        "gn_gain": jnp.clip(1.0 + 0.15 * jax.random.normal(splits[5], (C,), jnp.float32), 0.25, 1.75),
        "ln_gain": jnp.clip(1.0 + 0.15 * jax.random.normal(splits[6], (C,), jnp.float32), 0.25, 1.75),
        "time_scale": scatter_about(splits[7], (C,), 1.0, 4.0, (), jnp.float32),
        "conv_weight": scatter_about(splits[8], (3, 3, C, C), (9 * C) ** -0.5, 0.078125),
        "q_weight": draw_q_weight(jax.random.fold_in(splits[12], 71), part),
        "kv_weight": draw_kv_weight(jax.random.fold_in(splits[12], 71), part),
        "out_weight": scatter_about(splits[11], (C, C), C ** -0.5, 0.25),
    }


def alpha_bars():
    betas = jnp.linspace(0.00085 ** 0.5, 0.012 ** 0.5, 1000, dtype=jnp.float32) ** 2
    return jnp.cumprod(1.0 - betas)

def table_pick(table, index):
    places = jnp.arange(table.shape[0], dtype=jnp.int32)
    return jnp.sum(jnp.where(places == index, table, jnp.zeros_like(table)))

def sinusoid(step_value, width):
    half = width // 2
    freqs = jnp.exp(-math.log(10000.0) * jnp.arange(half, dtype=jnp.float32) / half)
    angles = step_value.astype(jnp.float32) * freqs
    return jnp.concatenate([jnp.cos(angles), jnp.sin(angles)])

def update_coeffs(t_now, t_next):
    table = alpha_bars()
    now = table_pick(table, t_now)
    after = table_pick(table, t_next)
    keep = jnp.sqrt(after / now)
    blend = jnp.sqrt(1.0 - after) - jnp.sqrt(after) * jnp.sqrt(1.0 - now) / jnp.sqrt(now)
    return (keep, blend)

def group_silu(field, gain):
    rows, cols, width = field.shape
    grouped = field.reshape(rows, cols, GROUPS, width // GROUPS)
    mean = lax.optimization_barrier(jnp.mean(grouped, axis=(0, 1, 3), keepdims=True))
    centered = grouped - mean
    var = lax.optimization_barrier(jnp.mean(centered * centered, axis=(0, 1, 3), keepdims=True))
    normed = (centered / jnp.sqrt(var + 1e-05)).reshape(rows, cols, width) * gain
    return jax.nn.silu(normed).astype(jnp.bfloat16)

def layer_norm(field, gain):
    mean = lax.optimization_barrier(jnp.mean(field, axis=-1, keepdims=True))
    centered = field - mean
    var = lax.optimization_barrier(jnp.mean(centered * centered, axis=-1, keepdims=True))
    return (centered / jnp.sqrt(var + 1e-05) * gain).astype(jnp.bfloat16)

def wide_rows(field):
    cols = field.shape[1]
    padded = jnp.pad(field, ((0, 0), (1, 1), (0, 0)))
    return jnp.concatenate([padded[:, 0:cols], padded[:, 1:cols + 1], padded[:, 2:cols + 2]], axis=-1)

def convolve_ref(fresh, stale, weight):
    rows, cols, width = fresh.shape
    zero_row = jnp.zeros((1, cols, width), fresh.dtype)
    fresh_above = jnp.concatenate([zero_row, fresh[:-1]], axis=0)
    stale_above = jnp.concatenate([zero_row, stale[:-1]], axis=0)
    fresh_below = jnp.concatenate([fresh[1:], zero_row], axis=0)
    stale_below = jnp.concatenate([stale[1:], zero_row], axis=0)
    place = jnp.arange(rows, dtype=jnp.int32) % ROWS_DEV
    above = jnp.where((place == 0)[:, None, None], stale_above, fresh_above)
    below = jnp.where((place == ROWS_DEV - 1)[:, None, None], stale_below, fresh_below)
    taps = weight.reshape(3, 3 * width, width)
    total = jnp.zeros((rows * cols, width), jnp.float32)
    for tap_row, source in enumerate([above, fresh, below]):
        total = total + jnp.dot(wide_rows(source).reshape(-1, 3 * width), taps[tap_row], preferred_element_type=jnp.float32)
    return total.reshape(rows, cols, width)

def attend_ref(fresh, stale, q_weight, kv_weight, out_weight):
    rows, cols, width = fresh.shape
    per_patch = ROWS_DEV * cols
    query = jnp.dot(fresh.reshape(-1, width), q_weight, preferred_element_type=jnp.float32).astype(jnp.bfloat16)
    fresh_kv = jnp.dot(fresh.reshape(-1, width), kv_weight, preferred_element_type=jnp.float32).astype(jnp.bfloat16)
    stale_kv = jnp.dot(stale.reshape(-1, width), kv_weight, preferred_element_type=jnp.float32).astype(jnp.bfloat16)
    key_patch = jnp.arange(rows * cols, dtype=jnp.int32) // per_patch

    def one_patch(patch_index):
        block = lax.dynamic_slice_in_dim(query, (patch_index * per_patch).astype(jnp.int32), per_patch, 0)
        block = block.reshape(per_patch, HEADS, HEAD_DIM).astype(jnp.float32)
        chosen = jnp.where((key_patch == patch_index)[:, None], fresh_kv, stale_kv)
        keys = chosen[:, :width].reshape(-1, HEADS, HEAD_DIM).astype(jnp.float32)
        values = chosen[:, width:].reshape(-1, HEADS, HEAD_DIM).astype(jnp.float32)
        scores = jnp.einsum('qhd,khd->hqk', block, keys) * HEAD_DIM ** (-0.5)
        weights = jnp.exp(scores - lax.optimization_barrier(jnp.max(scores, axis=-1, keepdims=True)))
        totals = lax.optimization_barrier(jnp.sum(weights, axis=-1))
        probs = weights.astype(jnp.bfloat16).astype(jnp.float32)
        mixed = jnp.einsum('hqk,khd->qhd', probs, values) / jnp.transpose(totals)[:, :, None]
        mixed = mixed.astype(jnp.bfloat16).reshape(per_patch, width)
        return jnp.dot(mixed, out_weight, preferred_element_type=jnp.float32)
    outputs = lax.map(one_patch, jnp.arange(rows // ROWS_DEV, dtype=jnp.int32))
    return outputs.reshape(rows, cols, width)

def reference(latent, stale_conv, stale_attn, cond_embed, timesteps, gn_gain, ln_gain, time_scale, conv_weight, q_weight, kv_weight, out_weight):
    state = latent
    width = latent.shape[2]
    prev_conv = [stale_conv[0], stale_conv[1]]
    prev_attn = [stale_attn[0], stale_attn[1]]
    guided = jnp.zeros_like(latent)
    for step in range(STEPS):
        conv_in = group_silu(state, gn_gain)
        predictions = []
        next_attn = []
        for branch in range(2):
            temb = jax.nn.silu(time_scale * sinusoid(timesteps[step], width) + cond_embed[branch])
            hidden = state + convolve_ref(conv_in, prev_conv[branch], conv_weight) + temb
            attn_in = layer_norm(hidden, ln_gain)
            predictions.append(hidden + attend_ref(attn_in, prev_attn[branch], q_weight, kv_weight, out_weight))
            next_attn.append(attn_in)
        guided = predictions[0] + 3.0 * (predictions[1] - predictions[0])
        keep, blend = update_coeffs(timesteps[step], timesteps[step + 1])
        state = keep * state + blend * guided
        prev_conv = [conv_in, conv_in]
        prev_attn = next_attn
    return (state, guided)
```

```python
import functools
import math

import jax
import jax.numpy as jnp
import numpy as np
from jax import lax
from jax.experimental import pallas as pl
from jax.experimental.pallas import tpu as pltpu
from jax.sharding import PartitionSpec as P

HEADS = 10
GROUPS = 32
STEPS = 2
PATCHES = 8
COLS = 128
WIDTH = 640
PAIRS = HEADS // 2
PER_GROUP = WIDTH // GROUPS
BF = jnp.bfloat16
F32 = jnp.float32
EXACT = lax.Precision.HIGHEST


def alpha_table():
    start, stop = np.float32(0.00085**0.5), np.float32(0.012**0.5)
    betas = np.linspace(start, stop, 1000, dtype=np.float32) ** 2
    return np.cumprod(1.0 - betas.astype(np.float64)).astype(np.float32)


def table_pick(table, index):
    places = jnp.arange(table.shape[0], dtype=jnp.int32)
    return jnp.sum(jnp.where(places == index, table, jnp.zeros_like(table)))


def sinusoid(step_value, width):
    half = width // 2
    freqs = jnp.exp(-math.log(10000.0) * jnp.arange(half, dtype=F32) / half)
    angles = step_value.astype(F32) * freqs
    return jnp.concatenate([jnp.cos(angles), jnp.sin(angles)])


def update_coeffs(t_now, t_next):
    table = jnp.asarray(alpha_table())
    now = table_pick(table, t_now)
    after = table_pick(table, t_next)
    keep = jnp.sqrt(after / now)
    blend = jnp.sqrt(1.0 - after) - jnp.sqrt(after) * jnp.sqrt(1.0 - now) / jnp.sqrt(now)
    return (keep, blend)


def dot(a, b):
    return jnp.dot(a, b, preferred_element_type=F32)


def dot_exact(a, b):
    return jnp.dot(a, b, preferred_element_type=F32, precision=EXACT)


def call(body, outs, *args, scratch=(), flops=0, traffic=0):
    specs = []
    for arg in args:
        small = arg.ndim == 1 and arg.shape[0] <= 8
        specs.append(pl.BlockSpec(memory_space=pltpu.SMEM if small else pltpu.VMEM))
    return pl.pallas_call(
        body,
        out_shape=outs,
        in_specs=specs,
        out_specs=jax.tree.map(lambda _: pl.BlockSpec(memory_space=pltpu.VMEM), outs),
        scratch_shapes=list(scratch),
        compiler_params=pltpu.CompilerParams(vmem_limit_bytes=28 * 2**20),
        cost_estimate=pl.CostEstimate(flops=flops, bytes_accessed=traffic, transcendentals=0),
    )(*args)


def shape(dims, dtype):
    return jax.ShapeDtypeStruct(dims, dtype)


def group_matrix():
    channel = lax.broadcasted_iota(jnp.int32, (WIDTH, 128), 0)
    group = lax.broadcasted_iota(jnp.int32, (WIDTH, 128), 1)
    inside = (channel >= group * PER_GROUP) & (channel < (group + 1) * PER_GROUP)
    return jnp.where(inside, 1.0, 0.0).astype(F32)


def spread_matrix():
    group = lax.broadcasted_iota(jnp.int32, (128, WIDTH), 0)
    channel = lax.broadcasted_iota(jnp.int32, (128, WIDTH), 1)
    inside = (channel >= group * PER_GROUP) & (channel < (group + 1) * PER_GROUP)
    return jnp.where(inside, 1.0, 0.0).astype(F32)


def local_stats(x, stats_ref):
    gather, spread = group_matrix(), spread_matrix()
    mean_c = jnp.mean(x, axis=0, keepdims=True)
    centered = x - mean_c
    dev_c = jnp.sum(centered * centered, axis=0, keepdims=True)
    wide = lambda row: jnp.broadcast_to(row, (8, row.shape[1]))
    mean_g = dot_exact(wide(mean_c), gather) * (1.0 / PER_GROUP)
    off = wide(mean_c) - dot_exact(mean_g, spread)
    dev_g = dot_exact(wide(dev_c) + COLS * (off * off), gather)
    both = jnp.concatenate([mean_g[:1], dev_g[:1]], axis=0)
    stats_ref[...] = jnp.broadcast_to(both[None], stats_ref.shape)


def first_body(x_ref, attn_ref, conv_ref, stats_ref, out_ref):
    out_ref[0] = attn_ref[0, 0]
    out_ref[1] = conv_ref[0, 0]
    local_stats(x_ref[0], stats_ref)


def shifted(x):
    place = lax.broadcasted_iota(jnp.int32, x.shape, 0)
    before = jnp.where(place == 0, 0.0, pltpu.roll(x, 1, 0))
    after = jnp.where(place == COLS - 1, 0.0, pltpu.roll(x, COLS - 1, 0))
    return before, after


def conv_row(x, weights):
    before, after = shifted(x)
    return (
        dot(before.astype(BF), weights[0])
        + dot(x.astype(BF), weights[1])
        + dot(after.astype(BF), weights[2])
    )


def rims_body(edge_ref, up_ref, down_ref, w_ref, out_ref):
    above = up_ref[1].astype(F32) * edge_ref[0]
    below = down_ref[1].astype(F32) * edge_ref[1]
    out_ref[...] = conv_row(above, w_ref[0]) + conv_row(below, w_ref[2])


def level_body(
    stats_ref, x_ref, rims_ref, temb_ref, gn_ref, ln_ref, w_ref, q_ref, pair_ref, h_ref, query_ref
):
    mean = jnp.zeros((1, 128), F32)
    for p in range(PATCHES):
        mean = mean + stats_ref[p, 0:1]
    mean = mean * (1.0 / PATCHES)
    dev = jnp.zeros((1, 128), F32)
    for p in range(PATCHES):
        off = stats_ref[p, 0:1] - mean
        dev = dev + stats_ref[p, 1:2] + (COLS * PER_GROUP) * (off * off)
    scale = 1.0 / jnp.sqrt(dev * (1.0 / (PATCHES * COLS * PER_GROUP)) + 1e-05)
    rows = jnp.concatenate([jnp.broadcast_to(mean, (8, 128)), jnp.broadcast_to(scale, (8, 128))], axis=0)
    wide = dot_exact(rows, spread_matrix())
    x = x_ref[0]
    normed = (x - wide[0:1]) * (wide[8:9] * gn_ref[...])
    conv_in = normed * jax.nn.sigmoid(normed)
    hidden = x + (conv_row(conv_in, w_ref[0]) + rims_ref[...]) + temb_ref[...]
    pair_ref[1] = conv_in.astype(BF)
    h_ref[...] = hidden
    mid = jnp.mean(hidden, axis=1, keepdims=True)
    centered = hidden - mid
    var = jnp.mean(centered * centered, axis=1, keepdims=True)
    attn_in = (centered * (1.0 / jnp.sqrt(var + 1e-05)) * ln_ref[...]).astype(BF)
    pair_ref[0] = attn_in
    query_ref[...] = dot(attn_in, q_ref[...]).astype(BF)


def keys_body(count, *refs):
    w_ref, out_ref = refs[count], refs[count + 1]
    for i in range(count):
        ref = refs[i]
        rows = ref[0] if len(ref.shape) == 3 else ref[...]
        out_ref[i * COLS : (i + 1) * COLS] = dot(rows, w_ref[...]).astype(BF)


def attend_body(count, query_ref, h_ref, early_ref, *refs):
    kv_ref, out_w_ref, eps_ref, late_ref, mixed_ref = refs[count:]
    for i in range(count):
        ref = refs[i]
        rows = ref[0] if len(ref.shape) == 3 else ref[...]
        late_ref[i * COLS : (i + 1) * COLS] = dot(rows, kv_ref[...]).astype(BF)
    first_half = lax.broadcasted_iota(jnp.int32, (COLS, 128), 1) < WIDTH // HEADS
    for pair in range(PAIRS):
        lanes = slice(pair * 128, (pair + 1) * 128)
        values = slice(WIDTH + pair * 128, WIDTH + (pair + 1) * 128)
        query = query_ref[:, lanes]
        zero = jnp.zeros_like(query)
        stacked = jnp.concatenate(
            [jnp.where(first_half, query, zero), jnp.where(first_half, zero, query)], axis=0
        )
        scores = [
            lax.dot_general(
                stacked, ref[:, lanes], (((1,), (1,)), ((), ())), preferred_element_type=F32
            )
            * (WIDTH // HEADS) ** (-0.5)
            for ref in (early_ref, late_ref)
        ]
        top = jnp.maximum(
            jnp.max(scores[0], axis=1, keepdims=True), jnp.max(scores[1], axis=1, keepdims=True)
        )
        weights = [jnp.exp(s - top) for s in scores]
        total = jnp.sum(weights[0], axis=1, keepdims=True) + jnp.sum(weights[1], axis=1, keepdims=True)
        product = dot(weights[0].astype(BF), early_ref[:, values]) + dot(
            weights[1].astype(BF), late_ref[:, values]
        )
        product = product / total
        mixed_ref[:, lanes] = jnp.where(first_half, product[:COLS], product[COLS:]).astype(BF)
    eps_ref[...] = (h_ref[...] + dot(mixed_ref[...], out_w_ref[...])).astype(eps_ref.dtype)


def guide(branch, own, other):
    uncond = jnp.where(branch == 0, own, other)
    cond = jnp.where(branch == 0, other, own)
    return uncond + 3.0 * (cond - uncond)


def update_body(branch_ref, coeff_ref, x_ref, own_ref, other_ref, state_ref, stats_ref):
    guided = guide(branch_ref[0], own_ref[...].astype(F32), other_ref[...].astype(F32))
    state = coeff_ref[0] * x_ref[0] + coeff_ref[1] * guided
    state_ref[0] = state
    local_stats(state, stats_ref)


def last_body(branch_ref, coeff_ref, x_ref, own_ref, other_ref, state_ref, guided_ref):
    guided = guide(branch_ref[0], own_ref[...].astype(F32), other_ref[...].astype(F32))
    state_ref[0] = coeff_ref[0] * x_ref[0] + coeff_ref[1] * guided
    guided_ref[0] = guided


def shards(
    latent,
    stale_conv,
    stale_attn,
    cond_embed,
    timesteps,
    gn_gain,
    ln_gain,
    time_scale,
    conv_weight,
    q_weight,
    kv_weight,
    out_weight,
):
    branch = lax.axis_index("cfg").astype(jnp.int32).reshape(1)
    patch = lax.axis_index("patch")
    edges = jnp.stack([patch > 0, patch < PATCHES - 1]).astype(F32)
    upward = [(i, (i + 1) % PATCHES) for i in range(PATCHES)]
    downward = [(target, source) for source, target in upward]
    up = lambda x: lax.ppermute(x, "patch", upward)
    down = lambda x: lax.ppermute(x, "patch", downward)
    full = (COLS, WIDTH)
    stats_shape = shape((PATCHES, 2, 128), F32)
    coeffs = [jnp.stack(update_coeffs(timesteps[s], timesteps[s + 1])) for s in range(STEPS)]
    tembs = [
        jax.nn.silu(time_scale * sinusoid(timesteps[s], WIDTH) + cond_embed[0]).reshape(1, WIDTH)
        for s in range(STEPS)
    ]
    gn_gain, ln_gain = gn_gain.reshape(1, WIDTH), ln_gain.reshape(1, WIDTH)
    center = conv_weight[1:2]
    matmul = 2 * COLS * WIDTH * WIDTH

    state = latent
    stats, pair = call(
        first_body, (stats_shape, shape((2,) + full, BF)), state, stale_attn, stale_conv
    )
    for step in range(STEPS):
        ups, downs = [up(pair)], [down(pair)]
        stats = lax.all_to_all(stats, "patch", 0, 0)
        rims = call(
            rims_body, shape(full, F32), edges, ups[0], downs[0], conv_weight, flops=6 * matmul
        )
        ups.append(up(ups[0][0]))
        downs.append(down(downs[0][0]))
        ups.append(up(ups[1]))
        downs.append(down(downs[1]))
        ups.append(up(ups[2]))
        early = call(
            functools.partial(keys_body, 4),
            shape((4 * COLS, 2 * WIDTH), BF),
            ups[0],
            downs[0],
            ups[1],
            downs[1],
            kv_weight,
            flops=8 * matmul,
        )
        pair, hidden, query = call(
            level_body,
            (shape((2,) + full, BF), shape(full, F32), shape(full, BF)),
            stats,
            state,
            rims,
            tembs[step],
            gn_gain,
            ln_gain,
            center,
            q_weight,
            flops=4 * matmul,
        )
        eps = call(
            functools.partial(attend_body, 4),
            shape(full, BF),
            query,
            hidden,
            early,
            pair,
            ups[2],
            downs[2],
            ups[3],
            kv_weight,
            out_weight,
            scratch=(pltpu.VMEM((4 * COLS, 2 * WIDTH), BF), pltpu.VMEM(full, BF)),
            flops=20 * matmul,
        )
        other = lax.ppermute(eps, "cfg", [(0, 1), (1, 0)])
        if step + 1 < STEPS:
            state, stats = call(
                update_body,
                (shape((1,) + full, F32), stats_shape),
                branch,
                coeffs[step],
                state,
                eps,
                other,
            )
    whole = shape((1,) + full, F32)
    return call(last_body, (whole, whole), branch, coeffs[-1], state, eps, other)


def solution(mesh):
    placed = (
        P(("batch", "patch"), None, None),
        P("cfg", ("batch", "patch"), None, None),
        P("cfg", ("batch", "patch"), None, None),
        P(("batch", "cfg"), None),
        P(),
        P(),
        P(),
        P(),
        P(),
        P(),
        P(),
        P(),
    )
    return jax.shard_map(
        shards,
        mesh=mesh,
        in_specs=placed,
        out_specs=(P(("batch", "patch"), None, None), P(("batch", "patch"), None, None)),
        check_vma=False,
    )
```

```python
import functools
import math

import jax
import jax.numpy as jnp
import numpy as np
from jax import lax
from jax.experimental import pallas as pl
from jax.experimental.pallas import tpu as pltpu
from jax.sharding import PartitionSpec as P

HEADS = 10
GROUPS = 32
STEPS = 2
PATCHES = 8
COLS = 128
WIDTH = 640
PAIRS = HEADS // 2
PER_GROUP = WIDTH // GROUPS
BYTES_PER_MICRO = 3.4e6
BF = jnp.bfloat16
F32 = jnp.float32


def alpha_table():
    start, stop = np.float32(0.00085**0.5), np.float32(0.012**0.5)
    betas = np.linspace(start, stop, 1000, dtype=np.float32) ** 2
    return np.cumprod(1.0 - betas.astype(np.float64)).astype(np.float32)


def dot(a, b):
    return jnp.dot(a, b, preferred_element_type=F32)


def dot_exact(a, b):
    high = a.astype(BF)
    rest = a - high.astype(F32)
    mid = rest.astype(BF)
    low = (rest - mid.astype(F32)).astype(BF)
    return dot(high, b) + (dot(mid, b) + dot(low, b))


HBM, FAR, NEAR, VMEM, SCALARS = "hbm", "far", "near", "vmem", "scalars"


class Arriving:
    def __init__(self, source, target, sem):
        self.copy = pltpu.make_async_copy(source, target, sem)
        self.target, self.waiting, self.shape = target, True, target.shape
        self.copy.start()

    def wait(self):
        if self.waiting:
            self.copy.wait()
            self.waiting = False

    def __getitem__(self, index):
        self.wait()
        return self.target[index]


def call(body, outs, *args, scratch=(), after=(), micros=0.1, limit=12):
    args += tuple((one, "token") for one in after)
    count, far = len(args), [i for i, (_, where) in enumerate(args) if where in (HBM, NEAR)]
    leaves, tree = jax.tree.flatten(outs)
    specs = {
        HBM: pl.BlockSpec(memory_space=pl.ANY),
        FAR: pl.BlockSpec(memory_space=pl.ANY),
        NEAR: pl.BlockSpec(memory_space=pl.ANY),
        "token": pl.BlockSpec(memory_space=pl.ANY),
        VMEM: pl.BlockSpec(memory_space=pltpu.VMEM),
        SCALARS: pl.BlockSpec(memory_space=pltpu.SMEM),
    }
    buffers = [pltpu.VMEM(args[i][0].shape, args[i][0].dtype) for i in far]
    if far:
        buffers.append(pltpu.SemaphoreType.DMA((len(far),)))

    def wrapped(*refs):
        ins, rest = list(refs[:count]), list(refs[count:])
        if far:
            held, sem = rest[-len(buffers) : -1], rest[-1]
            rest = rest[: -len(buffers)]
            for k, i in enumerate(far):
                ins[i] = Arriving(ins[i], held[k], sem.at[k])
        body(*ins[: count - len(after)], *rest)
        for i in far:
            ins[i].wait()

    def put(arg, where):
        if where not in (VMEM, HBM, FAR):
            return arg
        return pltpu.with_memory_space_constraint(arg, pltpu.VMEM if where == VMEM else pltpu.HBM)

    return pl.pallas_call(
        wrapped,
        out_shape=jax.tree.unflatten(tree, leaves),
        in_specs=[specs[where] for _, where in args],
        out_specs=jax.tree.unflatten(tree, [specs[VMEM] for _ in leaves]),
        scratch_shapes=list(scratch) + buffers,
        compiler_params=pltpu.CompilerParams(vmem_limit_bytes=limit * 2**20),
        cost_estimate=pl.CostEstimate(
            flops=0, bytes_accessed=int(micros * BYTES_PER_MICRO), transcendentals=0
        ),
    )(*[put(arg, where) for arg, where in args])


def fast(dims, dtype):
    return pltpu.VMEM(dims, dtype)


def later(arrays, after):
    count = len(arrays)
    spec = pl.BlockSpec(memory_space=pl.ANY)
    return list(pl.pallas_call(
        lambda *refs: None,
        out_shape=[shape(one.shape, one.dtype) for one in arrays],
        in_specs=[spec] * (count + len(after)),
        out_specs=[spec] * count,
        input_output_aliases={i: i for i in range(count)},
        cost_estimate=pl.CostEstimate(flops=0, bytes_accessed=0, transcendentals=0),
        compiler_params=pltpu.CompilerParams(vmem_limit_bytes=2**20),
    )(*arrays, *after))


def shape(dims, dtype):
    return jax.ShapeDtypeStruct(dims, dtype)


def group_matrix():
    channel = lax.broadcasted_iota(jnp.int32, (WIDTH, 128), 0)
    group = lax.broadcasted_iota(jnp.int32, (WIDTH, 128), 1)
    inside = (channel >= group * PER_GROUP) & (channel < (group + 1) * PER_GROUP)
    return jnp.where(inside, 1.0, 0.0).astype(BF)


def spread_matrix():
    group = lax.broadcasted_iota(jnp.int32, (128, WIDTH), 0)
    channel = lax.broadcasted_iota(jnp.int32, (128, WIDTH), 1)
    inside = (channel >= group * PER_GROUP) & (channel < (group + 1) * PER_GROUP)
    return jnp.where(inside, 1.0, 0.0).astype(BF)


def local_stats(x):
    gather, spread = group_matrix(), spread_matrix()
    mean_c = jnp.mean(x, axis=0, keepdims=True)
    centered = x - mean_c
    dev_c = jnp.sum(centered * centered, axis=0, keepdims=True)
    wide = lambda row: jnp.broadcast_to(row, (8, row.shape[1]))
    mean_g = dot_exact(wide(mean_c), gather) * (1.0 / PER_GROUP)
    off = wide(mean_c) - dot_exact(mean_g, spread)
    dev_g = dot_exact(wide(dev_c) + COLS * (off * off), gather)
    return jnp.concatenate([mean_g[:1], dev_g[:1]], axis=0)


def load_body(*refs):
    count = (len(refs) - 8) // 2
    sources, small, out_ref = refs[:count], refs[count : count + 6], refs[count + 6]
    targets, sem = refs[count + 7 : -1], refs[-1]
    copies = [
        pltpu.make_async_copy(source, target, sem.at[k])
        for k, (source, target) in enumerate(zip(sources, targets))
    ]
    for copy in copies:
        copy.start()
    prep_body(*small, out_ref)
    for copy in copies:
        copy.wait()


def prep_body(steps_ref, table_ref, scale_ref, embed_ref, gn_ref, ln_ref, out_ref):
    half = WIDTH // 2
    lane = lax.broadcasted_iota(jnp.int32, (1, WIDTH), 1)
    low = lane < half
    index = jnp.where(low, lane, lane - half).astype(F32)
    freqs = jnp.exp(index * (-math.log(10000.0) / half))
    table = table_ref[...]
    places = lax.broadcasted_iota(jnp.int32, table.shape, 0) * 128 + lax.broadcasted_iota(
        jnp.int32, table.shape, 1
    )
    pick = lambda t: jnp.sum(jnp.where(places == t, table, 0.0), keepdims=True)
    steps = [steps_ref[0:1, s : s + 1] for s in range(STEPS + 1)]
    levels = [pick(t) for t in steps]
    row = lambda value: jnp.broadcast_to(value, (1, WIDTH))
    rows = []
    for s in range(STEPS):
        angles = steps[s].astype(F32) * freqs
        wave = jnp.where(low, jnp.cos(angles), jnp.sin(angles))
        rows.append(scale_ref[...].reshape(1, WIDTH) * wave + embed_ref[...])
    rows = [r * jax.nn.sigmoid(r) for r in rows]
    for s in range(STEPS):
        now, after = levels[s], levels[s + 1]
        rows.append(row(jnp.sqrt(after / now)))
        rows.append(
            row(jnp.sqrt(1.0 - after) - jnp.sqrt(after) * jnp.sqrt(1.0 - now) / jnp.sqrt(now))
        )
    rows.append(gn_ref[...].reshape(1, WIDTH))
    rows.append(ln_ref[...].reshape(1, WIDTH))
    for r, value in enumerate(rows):
        out_ref[r : r + 1] = value


GN_ROW, LN_ROW = 3 * STEPS, 3 * STEPS + 1


def first_body(x_ref, attn_ref, conv_ref, pair_ref, state_ref, stats_ref, sem):
    copies = [
        pltpu.make_async_copy(source, pair_ref.at[pl.ds(k * COLS, COLS)], sem.at[k])
        for k, source in enumerate((attn_ref, conv_ref))
    ]
    for copy in copies:
        copy.start()
    x = x_ref[...]
    state_ref[...] = x
    stats_ref[...] = jnp.broadcast_to(local_stats(x[0])[None], stats_ref.shape)
    for copy in copies:
        copy.wait()


def trim_body(*refs):
    count = len(refs) // 2
    for source, target in zip(refs[:count], refs[count:]):
        target[...] = source[:COLS]


def shifted(x):
    place = lax.broadcasted_iota(jnp.int32, x.shape, 0)
    before = jnp.where(place == 0, 0.0, pltpu.roll(x, 1, 0))
    after = jnp.where(place == COLS - 1, 0.0, pltpu.roll(x, COLS - 1, 0))
    return before, after


def conv_row(x, taps):
    before, after = shifted(x)
    return (
        dot(x.astype(BF), taps[1][...])
        + dot(before.astype(BF), taps[0][...])
        + dot(after.astype(BF), taps[2][...])
    )


def rims_body(place_ref, up_ref, down_ref, w_ref, out_ref):
    above = up_ref[COLS:].astype(F32) * place_ref[0]
    below = down_ref[COLS:].astype(F32) * place_ref[1]
    out_ref[...] = conv_row(above, [w_ref[0, t] for t in range(3)]) + conv_row(
        below, [w_ref[2, t] for t in range(3)]
    )


def level(step, moments, x, rims, prep_ref, taps, q_w):
    mean, dev = moments
    scale = 1.0 / jnp.sqrt(dev * (1.0 / (PATCHES * COLS * PER_GROUP)) + 1e-05)
    rows = jnp.concatenate([jnp.broadcast_to(mean, (8, 128)), jnp.broadcast_to(scale, (8, 128))], axis=0)
    wide = dot_exact(rows, spread_matrix())
    x = x[0]
    normed = (x - wide[0:1]) * (wide[8:9] * prep_ref[GN_ROW : GN_ROW + 1])
    conv_in = normed * jax.nn.sigmoid(normed)
    hidden = x + (conv_row(conv_in, taps) + rims[...]) + prep_ref[step : step + 1]
    mid = jnp.mean(hidden, axis=1, keepdims=True)
    centered = hidden - mid
    var = jnp.mean(centered * centered, axis=1, keepdims=True)
    attn_in = (centered * (1.0 / jnp.sqrt(var + 1e-05)) * prep_ref[LN_ROW : LN_ROW + 1]).astype(BF)
    scale = (WIDTH // HEADS) ** (-0.5) * math.log2(math.e)
    query = (dot(attn_in, q_w[...]) * scale).astype(BF)
    return conv_in.astype(BF), hidden, attn_in, query


def combined(stats):
    mean = sum(stats[p, 0:1] for p in range(PATCHES)) * (1.0 / PATCHES)
    dev = sum(stats[p, 1:2] for p in range(PATCHES))
    for p in range(PATCHES):
        off = stats[p, 0:1] - mean
        dev = dev + (COLS * PER_GROUP) * (off * off)
    return mean, dev


def level_body(stats_ref, x_ref, rims_ref, prep_ref, w_ref, q_ref, pair_ref, h_ref, query_ref):
    taps = [w_ref.at[1, t] for t in range(3)]
    pair_ref[COLS:], h_ref[...], pair_ref[:COLS], query_ref[...] = level(
        0, combined(stats_ref[...]), x_ref[...], rims_ref, prep_ref, taps, q_ref
    )


def keys_of(rows, kv_ref, out_ref):
    out_ref[...] = dot(jnp.concatenate([ref[:COLS] for ref in rows], axis=0), kv_ref[...]).astype(BF)


def keys_body(*refs):
    keys_of(refs[:-2], *refs[-2:])


def attend(query_ref, parts, mixed_ref):
    first_half = lax.broadcasted_iota(jnp.int32, (COLS, 128), 1) < WIDTH // HEADS
    for pair in range(PAIRS):
        lanes = slice(pair * 128, (pair + 1) * 128)
        values = slice(WIDTH + pair * 128, WIDTH + (pair + 1) * 128)
        query = query_ref[:, lanes]
        zero = jnp.zeros_like(query)
        stacked = jnp.concatenate(
            [jnp.where(first_half, query, zero), jnp.where(first_half, zero, query)], axis=0
        )
        scores = [
            lax.dot_general(
                stacked, ref[:, lanes], (((1,), (1,)), ((), ())), preferred_element_type=F32
            )
            for ref in parts
        ]
        top = functools.reduce(jnp.maximum, [jnp.max(s, axis=1, keepdims=True) for s in scores])
        weights = [jnp.exp2(s - top) for s in scores]
        total = sum(jnp.sum(w, axis=1, keepdims=True) for w in weights)
        product = sum(dot(w.astype(BF), ref[:, values]) for w, ref in zip(weights, parts))
        product = product * (1.0 / total)
        mixed_ref[:, lanes] = jnp.where(first_half, product[:COLS], product[COLS:]).astype(BF)


def attend_body(early, late, query_ref, h_ref, *refs):
    parts, rows = refs[:early], refs[early : early + 1 + late]
    kv_ref, out_w_ref, eps_ref, late_ref, mixed_ref = refs[early + 1 + late :]
    keys_of(rows, kv_ref, late_ref)
    attend(query_ref, (*parts, late_ref), mixed_ref)
    eps_ref[...] = (h_ref[...] + dot(mixed_ref[...], out_w_ref[...])).astype(eps_ref.dtype)


def second_body(stats_ref, x_ref, w_ref, rims_ref, prep_ref, q_ref, kv_ref, o_ref, *refs):
    attn_in_ref, h_ref, query_ref, kv_w, out_w, held_ref, sem, more_sem = refs
    taps = {t: Arriving(w_ref.at[1, t], held_ref.at[t], sem.at[t]) for t in (1, 0, 2)}
    copies = [
        pltpu.make_async_copy(source, target, more_sem.at[k])
        for k, (source, target) in enumerate(((kv_ref, kv_w), (o_ref, out_w)))
    ]
    for copy in copies:
        copy.start()
    _, h_ref[...], attn_in_ref[...], query_ref[...] = level(
        1, combined(stats_ref[...]), x_ref[...], rims_ref, prep_ref, taps, q_ref
    )
    for copy in copies:
        copy.wait()


def guide(place_ref, own_ref, other_ref):
    own, other = own_ref[...].astype(F32), other_ref[...].astype(F32)
    first = place_ref[2] == 0.0
    uncond = jnp.where(first, own, other)
    cond = jnp.where(first, other, own)
    return uncond + 3.0 * (cond - uncond)


def update_body(step, place_ref, prep_ref, x_ref, own_ref, other_ref, state_ref, *refs):
    guided = guide(place_ref, own_ref, other_ref)
    prep, row = prep_ref[...], STEPS + 2 * step
    state = prep[row : row + 1] * x_ref[0] + prep[row + 1 : row + 2] * guided
    state_ref[0] = state
    if step + 1 < STEPS:
        refs[0][...] = jnp.broadcast_to(local_stats(state)[None], refs[0].shape)
    else:
        refs[0][0] = guided


def shards(
    latent,
    stale_conv,
    stale_attn,
    cond_embed,
    timesteps,
    gn_gain,
    ln_gain,
    time_scale,
    conv_weight,
    q_weight,
    kv_weight,
    out_weight,
):
    patch, branch = lax.axis_index("patch"), lax.axis_index("cfg")
    place = jnp.stack([patch > 0, patch < PATCHES - 1, branch > 0]).astype(F32)
    upward = [(i, (i + 1) % PATCHES) for i in range(PATCHES)]
    downward = [(target, source) for source, target in upward]
    up = lambda x: lax.ppermute(x, "patch", upward)
    down = lambda x: lax.ppermute(x, "patch", downward)
    full = (COLS, WIDTH)
    whole = (1,) + full
    stats_shape = shape((PATCHES, 2, 128), F32)
    near = lambda arrays: [(one, NEAR) for one in arrays]
    gather_stats = lambda x: lax.all_to_all(x, "patch", 0, 0)

    pair, state, stats = call(
        first_body,
        (fast((2 * COLS, WIDTH), BF), fast(whole, F32), stats_shape),
        (latent, HBM),
        (stale_attn.reshape(full), FAR),
        (stale_conv.reshape(full), FAR),
        scratch=(pltpu.SemaphoreType.DMA((2,)),),
        after=(place,),
    )
    table = np.ones((8, 128), np.float32)
    table.reshape(-1)[:1000] = alpha_table()
    weights = (conv_weight, q_weight, kv_weight, out_weight)
    trim = lambda blocks, after=(): call(
        trim_body,
        tuple(fast(full, BF) for _ in blocks),
        *[(one, VMEM) for one in blocks],
        after=after,
    )

    ring1 = [up(pair), down(pair)]
    stats = gather_stats(stats)
    passing = trim(ring1, (stats,))
    ring2 = [up(passing[0]), down(passing[1])]
    prep, conv_w, q_w, kv_w, out_w = call(
        load_body,
        (fast((8, WIDTH), F32),) + tuple(fast(w.shape, w.dtype) for w in weights),
        *[(w, FAR) for w in weights],
        (timesteps.reshape(1, -1), HBM),
        (jnp.asarray(table), HBM),
        (time_scale, HBM),
        (cond_embed, HBM),
        (gn_gain, HBM),
        (ln_gain, HBM),
        scratch=(pltpu.SemaphoreType.DMA((4,)),),
        after=(stats,),
        limit=2,
    )
    keys = lambda blocks, after=(), micros=0.1: call(
        keys_body,
        fast((len(blocks) * COLS, 2 * WIDTH), BF),
        *near(blocks),
        (kv_w, VMEM),
        after=after,
        micros=micros,
    )
    conv_rims = lambda after=(), micros=0.1: call(
        rims_body,
        fast(full, F32),
        (place, SCALARS),
        *[(one, VMEM) for one in ring1],
        (conv_w, VMEM),
        after=after,
        micros=micros,
    )
    rims = conv_rims()
    ring2 = later(ring2, (prep,))
    ring3 = [up(ring2[0]), down(ring2[1])]
    pair, hidden, query = call(
        level_body,
        (fast((2 * COLS, WIDTH), BF), fast(full, F32), fast(full, BF)),
        (stats, VMEM),
        (state, VMEM),
        (rims, VMEM),
        (prep, VMEM),
        (conv_w, VMEM),
        (q_w, VMEM),
    )
    near_keys = keys(ring1, (rims,))
    ring3 = later(ring3, (near_keys,))
    ring4 = [up(ring3[0])]
    mid_keys = keys(ring2, (ring3[0],))
    far_keys = keys(ring3, (mid_keys,))
    ring1 = [up(pair), down(pair)]
    attend_to = lambda weights, early, late: call(
        functools.partial(attend_body, len(early), len(late)),
        fast(full, BF),
        (query, VMEM),
        (hidden, VMEM),
        *early,
        (pair, VMEM),
        *near(late),
        *[(w, VMEM) for w in weights],
        scratch=(pltpu.VMEM(((1 + len(late)) * COLS, 2 * WIDTH), BF), pltpu.VMEM(full, BF)),
        micros=4.0,
    )
    early = [(one, VMEM) for one in (near_keys, mid_keys, far_keys)]
    eps = attend_to((kv_w, out_w), early, ring4)
    exchange = lambda x: lax.ppermute(x, "cfg", [(0, 1), (1, 0)])
    other = exchange(eps)
    passing = trim(ring1, (eps,))
    ring2 = [up(passing[0]), down(passing[1])]
    near_keys = keys(ring1, (passing[0],), 6.0)
    rims = conv_rims((near_keys,), 6.0)
    state, stats = call(
        functools.partial(update_body, 0),
        (fast(whole, F32), stats_shape),
        (place, SCALARS),
        (prep, VMEM),
        (state, VMEM),
        (eps, VMEM),
        (other, VMEM),
        after=(rims,),
    )
    ring2 = later(ring2, (state,))
    ring3 = [up(ring2[0]), down(ring2[1])]
    stats = gather_stats(stats)
    ring3 = later(ring3, (stats,))
    ring4 = [up(ring3[0])]
    pair, hidden, query, kv_w, out_w = call(
        second_body,
        (fast(full, BF), fast(full, F32), fast(full, BF))
        + tuple(fast(w.shape, w.dtype) for w in weights[2:]),
        (stats, NEAR),
        (state, NEAR),
        (conv_weight, FAR),
        (rims, NEAR),
        (prep, NEAR),
        (q_weight, HBM),
        (kv_weight, FAR),
        (out_weight, FAR),
        scratch=(
            pltpu.VMEM((3, WIDTH, WIDTH), BF),
            pltpu.SemaphoreType.DMA((3,)),
            pltpu.SemaphoreType.DMA((2,)),
        ),
        after=(ring3[0],),
    )
    mid_keys = keys(ring2)
    eps = attend_to((kv_w, out_w), [(near_keys, NEAR), (mid_keys, VMEM)], ring3 + ring4)
    other = exchange(eps)
    return call(
        functools.partial(update_body, 1),
        (shape(whole, F32), shape(whole, F32)),
        (place, SCALARS),
        (prep, VMEM),
        (state, VMEM),
        (eps, VMEM),
        (other, VMEM),
    )


def solution(mesh):
    placed = (
        P(("batch", "patch"), None, None),
        P("cfg", ("batch", "patch"), None, None),
        P("cfg", ("batch", "patch"), None, None),
        P(("batch", "cfg"), None),
        P(),
        P(),
        P(),
        P(),
        P(),
        P(),
        P(),
        P(),
    )
    return jax.shard_map(
        shards,
        mesh=mesh,
        in_specs=placed,
        out_specs=(P(("batch", "patch"), None, None), P(("batch", "patch"), None, None)),
        check_vma=False,
    )
```

```python
import functools
import math

import jax
import jax.numpy as jnp
import numpy as np
from jax import lax
from jax.experimental import pallas as pl
from jax.experimental.pallas import tpu as pltpu
from jax.sharding import PartitionSpec as P

HEADS = 10
GROUPS = 32
STEPS = 2
PATCHES = 8
COLS = 128
WIDTH = 640
PAIRS = HEADS // 2
PER_GROUP = WIDTH // GROUPS
BYTES_PER_MICRO = 3.4e6
BF = jnp.bfloat16
F32 = jnp.float32


def alpha_table():
    start, stop = np.float32(0.00085**0.5), np.float32(0.012**0.5)
    betas = np.linspace(start, stop, 1000, dtype=np.float32) ** 2
    return np.cumprod(1.0 - betas.astype(np.float64)).astype(np.float32)


def dot(a, b):
    return jnp.dot(a, b, preferred_element_type=F32)


def dot_exact(a, b):
    high = a.astype(BF)
    rest = a - high.astype(F32)
    mid = rest.astype(BF)
    low = (rest - mid.astype(F32)).astype(BF)
    return dot(high, b) + (dot(mid, b) + dot(low, b))


HBM, FAR, NEAR, VMEM, SCALARS = "hbm", "far", "near", "vmem", "scalars"


class Arriving:
    def __init__(self, source, target, sem):
        self.copy = pltpu.make_async_copy(source, target, sem)
        self.target, self.waiting, self.shape = target, True, target.shape
        self.copy.start()

    def wait(self):
        if self.waiting:
            self.copy.wait()
            self.waiting = False

    def __getitem__(self, index):
        self.wait()
        return self.target[index]


def call(body, outs, *args, scratch=(), after=(), micros=0.1, limit=12):
    args += tuple((one, "token") for one in after)
    count, far = len(args), [i for i, (_, where) in enumerate(args) if where in (HBM, NEAR)]
    leaves, tree = jax.tree.flatten(outs)
    specs = {
        HBM: pl.BlockSpec(memory_space=pl.ANY),
        FAR: pl.BlockSpec(memory_space=pl.ANY),
        NEAR: pl.BlockSpec(memory_space=pl.ANY),
        "token": pl.BlockSpec(memory_space=pl.ANY),
        VMEM: pl.BlockSpec(memory_space=pltpu.VMEM),
        SCALARS: pl.BlockSpec(memory_space=pltpu.SMEM),
    }
    buffers = [pltpu.VMEM(args[i][0].shape, args[i][0].dtype) for i in far]
    if far:
        buffers.append(pltpu.SemaphoreType.DMA((len(far),)))

    def wrapped(*refs):
        ins, rest = list(refs[:count]), list(refs[count:])
        if far:
            held, sem = rest[-len(buffers) : -1], rest[-1]
            rest = rest[: -len(buffers)]
            for k, i in enumerate(far):
                ins[i] = Arriving(ins[i], held[k], sem.at[k])
        body(*ins[: count - len(after)], *rest)
        for i in far:
            ins[i].wait()

    def put(arg, where):
        if where not in (VMEM, HBM, FAR):
            return arg
        return pltpu.with_memory_space_constraint(arg, pltpu.VMEM if where == VMEM else pltpu.HBM)

    return pl.pallas_call(
        wrapped,
        out_shape=jax.tree.unflatten(tree, leaves),
        in_specs=[specs[where] for _, where in args],
        out_specs=jax.tree.unflatten(tree, [specs[VMEM] for _ in leaves]),
        scratch_shapes=list(scratch) + buffers,
        compiler_params=pltpu.CompilerParams(vmem_limit_bytes=limit * 2**20),
        cost_estimate=pl.CostEstimate(
            flops=0, bytes_accessed=int(micros * BYTES_PER_MICRO), transcendentals=0
        ),
    )(*[put(arg, where) for arg, where in args])


def fast(dims, dtype):
    return pltpu.VMEM(dims, dtype)


def later(arrays, after):
    count = len(arrays)
    spec = pl.BlockSpec(memory_space=pl.ANY)
    return list(pl.pallas_call(
        lambda *refs: None,
        out_shape=[shape(one.shape, one.dtype) for one in arrays],
        in_specs=[spec] * (count + len(after)),
        out_specs=[spec] * count,
        input_output_aliases={i: i for i in range(count)},
        cost_estimate=pl.CostEstimate(flops=0, bytes_accessed=0, transcendentals=0),
        compiler_params=pltpu.CompilerParams(vmem_limit_bytes=2**20),
    )(*arrays, *after))


def shape(dims, dtype):
    return jax.ShapeDtypeStruct(dims, dtype)


def group_matrix():
    channel = lax.broadcasted_iota(jnp.int32, (WIDTH, 128), 0)
    group = lax.broadcasted_iota(jnp.int32, (WIDTH, 128), 1)
    inside = (channel >= group * PER_GROUP) & (channel < (group + 1) * PER_GROUP)
    return jnp.where(inside, 1.0, 0.0).astype(BF)


def spread_matrix():
    group = lax.broadcasted_iota(jnp.int32, (128, WIDTH), 0)
    channel = lax.broadcasted_iota(jnp.int32, (128, WIDTH), 1)
    inside = (channel >= group * PER_GROUP) & (channel < (group + 1) * PER_GROUP)
    return jnp.where(inside, 1.0, 0.0).astype(BF)


def local_stats(x):
    gather, spread = group_matrix(), spread_matrix()
    mean_c = jnp.mean(x, axis=0, keepdims=True)
    centered = x - mean_c
    dev_c = jnp.sum(centered * centered, axis=0, keepdims=True)
    wide = lambda row: jnp.broadcast_to(row, (8, row.shape[1]))
    mean_g = dot_exact(wide(mean_c), gather) * (1.0 / PER_GROUP)
    off = wide(mean_c) - dot_exact(mean_g, spread)
    dev_g = dot_exact(wide(dev_c) + COLS * (off * off), gather)
    return jnp.concatenate([mean_g[:1], dev_g[:1]], axis=0)


def load_body(*refs):
    count = (len(refs) - 8) // 2
    sources, small, out_ref = refs[:count], refs[count : count + 6], refs[count + 6]
    targets, sem = refs[count + 7 : -1], refs[-1]
    copies = [
        pltpu.make_async_copy(source, target, sem.at[k])
        for k, (source, target) in enumerate(zip(sources, targets))
    ]
    for copy in copies:
        copy.start()
    prep_body(*small, out_ref)
    for copy in copies:
        copy.wait()


def prep_body(steps_ref, table_ref, scale_ref, embed_ref, gn_ref, ln_ref, out_ref):
    half = WIDTH // 2
    lane = lax.broadcasted_iota(jnp.int32, (1, WIDTH), 1)
    low = lane < half
    index = jnp.where(low, lane, lane - half).astype(F32)
    freqs = jnp.exp(index * (-math.log(10000.0) / half))
    table = table_ref[...]
    places = lax.broadcasted_iota(jnp.int32, table.shape, 0) * 128 + lax.broadcasted_iota(
        jnp.int32, table.shape, 1
    )
    pick = lambda t: jnp.sum(jnp.where(places == t, table, 0.0), keepdims=True)
    steps = [steps_ref[0:1, s : s + 1] for s in range(STEPS + 1)]
    levels = [pick(t) for t in steps]
    row = lambda value: jnp.broadcast_to(value, (1, WIDTH))
    rows = []
    for s in range(STEPS):
        angles = steps[s].astype(F32) * freqs
        wave = jnp.where(low, jnp.cos(angles), jnp.sin(angles))
        rows.append(scale_ref[...].reshape(1, WIDTH) * wave + embed_ref[...])
    rows = [r * jax.nn.sigmoid(r) for r in rows]
    for s in range(STEPS):
        now, after = levels[s], levels[s + 1]
        rows.append(row(jnp.sqrt(after / now)))
        rows.append(
            row(jnp.sqrt(1.0 - after) - jnp.sqrt(after) * jnp.sqrt(1.0 - now) / jnp.sqrt(now))
        )
    rows.append(gn_ref[...].reshape(1, WIDTH))
    rows.append(ln_ref[...].reshape(1, WIDTH))
    for r, value in enumerate(rows):
        out_ref[r : r + 1] = value


GN_ROW, LN_ROW = 3 * STEPS, 3 * STEPS + 1
EXTRA = 16
HEAD = COLS + EXTRA


def stats_rows(stats):
    parts = []
    for _ in range(3):
        part = stats.astype(BF).astype(F32)
        parts.append(part)
        stats = stats - part
    rows = jnp.concatenate(parts + [jnp.zeros((EXTRA - 6, 128), F32)], axis=0)
    return jnp.concatenate([rows, jnp.zeros((EXTRA, WIDTH - 128), F32)], axis=1).astype(BF)


def stats_of(block_ref):
    rows = block_ref[COLS:HEAD, :128].astype(F32)
    return rows[0:2] + rows[2:4] + rows[4:6]


def merge(one, other):
    (count_a, mean_a, dev_a), (count_b, mean_b, dev_b) = one, other
    count, off = count_a + count_b, mean_b - mean_a
    scale = COLS * PER_GROUP * count_a * count_b / count
    return count, mean_a + off * (count_b / count), dev_a + dev_b + scale * (off * off)


def patches(count, stats):
    return count, stats[0:1], stats[1:2]


def first_body(x_ref, attn_ref, conv_ref, block_ref, state_ref, stats_ref, sem):
    places = ((attn_ref, 0), (conv_ref, HEAD))
    copies = [
        pltpu.make_async_copy(source, block_ref.at[pl.ds(start, COLS)], sem.at[k])
        for k, (source, start) in enumerate(places)
    ]
    for copy in copies:
        copy.start()
    x = x_ref[...]
    state_ref[...] = x
    stats = local_stats(x[0])
    stats_ref[0:2] = stats
    block_ref[COLS:HEAD] = stats_rows(stats)
    for copy in copies:
        copy.wait()


def join_body(low_ref, up_ref, down_ref, up_block_ref, down_block_ref):
    for source, target in ((up_ref, up_block_ref), (down_ref, down_block_ref)):
        target[:COLS] = source[...]
        target[COLS:] = low_ref[...]


def pack_body(stats_ref, up_ref, down_ref, up_block_ref, down_block_ref):
    rows = stats_rows(stats_ref[0:2])
    for source, target in ((up_ref, up_block_ref), (down_ref, down_block_ref)):
        target[:COLS] = source[:COLS]
        target[COLS:] = rows


def partial_body(mine_ref, up_ref, down_ref, three_ref, two_ref):
    two = merge(patches(1, stats_of(up_ref)), patches(1, mine_ref[0:2]))
    three = merge(two, patches(1, stats_of(down_ref)))
    for (_, mean, dev), target in ((three, three_ref), (two, two_ref)):
        target[0:1], target[1:2] = mean, dev


def trim_body(rows, *refs):
    count = len(refs) // 2
    for source, target in zip(refs[:count], refs[count:]):
        target[...] = source[:rows]


def shifted(x):
    place = lax.broadcasted_iota(jnp.int32, x.shape, 0)
    before = jnp.where(place == 0, 0.0, pltpu.roll(x, 1, 0))
    after = jnp.where(place == COLS - 1, 0.0, pltpu.roll(x, COLS - 1, 0))
    return before, after


def conv_row(x, taps):
    before, after = shifted(x)
    return (
        dot(x.astype(BF), taps[1][...])
        + dot(before.astype(BF), taps[0][...])
        + dot(after.astype(BF), taps[2][...])
    )


def rims_body(start, place_ref, up_ref, down_ref, w_ref, out_ref):
    above = up_ref[start : start + COLS].astype(F32) * place_ref[0]
    below = down_ref[start : start + COLS].astype(F32) * place_ref[1]
    out_ref[...] = conv_row(above, [w_ref[0, t] for t in range(3)]) + conv_row(
        below, [w_ref[2, t] for t in range(3)]
    )


def level(step, moments, x, rims, prep_ref, taps, q_w):
    _, mean, dev = moments
    scale = 1.0 / jnp.sqrt(dev * (1.0 / (PATCHES * COLS * PER_GROUP)) + 1e-05)
    rows = jnp.concatenate([jnp.broadcast_to(mean, (8, 128)), jnp.broadcast_to(scale, (8, 128))], axis=0)
    wide = dot_exact(rows, spread_matrix())
    x = x[0]
    normed = (x - wide[0:1]) * (wide[8:9] * prep_ref[GN_ROW : GN_ROW + 1])
    conv_in = normed * jax.nn.sigmoid(normed)
    hidden = x + (conv_row(conv_in, taps) + rims[...]) + prep_ref[step : step + 1]
    mid = jnp.mean(hidden, axis=1, keepdims=True)
    centered = hidden - mid
    var = jnp.mean(centered * centered, axis=1, keepdims=True)
    attn_in = (centered * (1.0 / jnp.sqrt(var + 1e-05)) * prep_ref[LN_ROW : LN_ROW + 1]).astype(BF)
    scale = (WIDTH // HEADS) ** (-0.5) * math.log2(math.e)
    query = (dot(attn_in, q_w[...]) * scale).astype(BF)
    return conv_in.astype(BF), hidden, attn_in, query


def level_body(x_ref, rims_ref, prep_ref, w_ref, q_ref, *refs):
    opposite_ref, conv_in_ref, h_ref, attn_in_ref, query_ref = refs[PATCHES - 1 :]
    total = patches(1, opposite_ref[0:2])
    for ref in refs[: PATCHES - 1]:
        total = merge(total, patches(1, stats_of(ref)))
    taps = [w_ref.at[1, t] for t in range(3)]
    conv_in_ref[...], h_ref[...], attn_in_ref[...], query_ref[...] = level(
        0, total, x_ref[...], rims_ref, prep_ref, taps, q_ref
    )


def keys_of(rows, kv_ref, out_ref):
    out_ref[...] = dot(jnp.concatenate([ref[:COLS] for ref in rows], axis=0), kv_ref[...]).astype(BF)


def keys_body(*refs):
    keys_of(refs[:-2], *refs[-2:])


def attend(query_ref, parts, mixed_ref):
    first_half = lax.broadcasted_iota(jnp.int32, (COLS, 128), 1) < WIDTH // HEADS
    for pair in range(PAIRS):
        lanes = slice(pair * 128, (pair + 1) * 128)
        values = slice(WIDTH + pair * 128, WIDTH + (pair + 1) * 128)
        query = query_ref[:, lanes]
        zero = jnp.zeros_like(query)
        stacked = jnp.concatenate(
            [jnp.where(first_half, query, zero), jnp.where(first_half, zero, query)], axis=0
        )
        scores = [
            lax.dot_general(
                stacked, ref[:, lanes], (((1,), (1,)), ((), ())), preferred_element_type=F32
            )
            for ref in parts
        ]
        top = functools.reduce(jnp.maximum, [jnp.max(s, axis=1, keepdims=True) for s in scores])
        weights = [jnp.exp2(s - top) for s in scores]
        total = sum(jnp.sum(w, axis=1, keepdims=True) for w in weights)
        product = sum(dot(w.astype(BF), ref[:, values]) for w, ref in zip(weights, parts))
        product = product * (1.0 / total)
        mixed_ref[:, lanes] = jnp.where(first_half, product[:COLS], product[COLS:]).astype(BF)


def attend_body(early, late, query_ref, h_ref, *refs):
    parts, rows = refs[:early], refs[early : early + 1 + late]
    kv_ref, out_w_ref, eps_ref, late_ref, mixed_ref = refs[early + 1 + late :]
    keys_of(rows, kv_ref, late_ref)
    attend(query_ref, (*parts, late_ref), mixed_ref)
    eps_ref[...] = (h_ref[...] + dot(mixed_ref[...], out_w_ref[...])).astype(eps_ref.dtype)


def second_body(
    three_ref, before_ref, after_ref, x_ref, rims_ref, prep_ref, w_ref, q_ref, *refs
):
    attn_in_ref, h_ref, query_ref = refs
    total = merge(patches(3, three_ref[0:2]), patches(2, after_ref[0:2]))
    total = merge(total, patches(3, before_ref[0:2]))
    taps = [w_ref.at[1, t] for t in range(3)]
    _, h_ref[...], attn_in_ref[...], query_ref[...] = level(
        1, total, x_ref[...], rims_ref, prep_ref, taps, q_ref
    )


def guide(place_ref, own_ref, other_ref):
    own, other = own_ref[...].astype(F32), other_ref[...].astype(F32)
    first = place_ref[2] == 0.0
    uncond = jnp.where(first, own, other)
    cond = jnp.where(first, other, own)
    return uncond + 3.0 * (cond - uncond)


def update_body(step, place_ref, prep_ref, x_ref, own_ref, other_ref, state_ref, *refs):
    guided = guide(place_ref, own_ref, other_ref)
    prep, row = prep_ref[...], STEPS + 2 * step
    state = prep[row : row + 1] * x_ref[0] + prep[row + 1 : row + 2] * guided
    state_ref[0] = state
    if step + 1 < STEPS:
        refs[0][0:2] = local_stats(state)
    else:
        refs[0][0] = guided


def shards(
    latent,
    stale_conv,
    stale_attn,
    cond_embed,
    timesteps,
    gn_gain,
    ln_gain,
    time_scale,
    conv_weight,
    q_weight,
    kv_weight,
    out_weight,
):
    patch, branch = lax.axis_index("patch"), lax.axis_index("cfg")
    place = jnp.stack([patch > 0, patch < PATCHES - 1, branch > 0]).astype(F32)
    upward = [(i, (i + 1) % PATCHES) for i in range(PATCHES)]
    downward = [(target, source) for source, target in upward]
    up = lambda x: lax.ppermute(x, "patch", upward)
    down = lambda x: lax.ppermute(x, "patch", downward)
    full = (COLS, WIDTH)
    whole = (1,) + full
    stats_shape = fast((8, 128), F32)
    near = lambda arrays: [(one, NEAR) for one in arrays]
    shift = lambda x, far: lax.ppermute(
        x, "patch", [(i, (i + far) % PATCHES) for i in range(PATCHES)]
    )

    first, state, opposite = call(
        first_body,
        (fast((HEAD + COLS, WIDTH), BF), fast(whole, F32), fast((8, 128), F32)),
        (latent, HBM),
        (stale_attn.reshape(full), FAR),
        (stale_conv.reshape(full), FAR),
        scratch=(pltpu.SemaphoreType.DMA((2,)),),
        after=(place,),
    )
    table = np.ones((8, 128), np.float32)
    table.reshape(-1)[:1000] = alpha_table()
    weights = (conv_weight, q_weight, kv_weight, out_weight)
    trim = lambda rows, blocks, after=(): call(
        functools.partial(trim_body, rows),
        tuple(fast((rows, WIDTH), BF) for _ in blocks),
        *[(one, VMEM) for one in blocks],
        after=after,
    )

    ring1 = [up(first), down(first)]
    opposite = shift(opposite, PATCHES // 2)
    prep, conv_w, q_w, kv_w, out_w = call(
        load_body,
        (fast((8, WIDTH), F32),) + tuple(fast(w.shape, w.dtype) for w in weights),
        *[(w, FAR) for w in weights],
        (timesteps.reshape(1, -1), HBM),
        (jnp.asarray(table), HBM),
        (time_scale, HBM),
        (cond_embed, HBM),
        (gn_gain, HBM),
        (ln_gain, HBM),
        scratch=(pltpu.SemaphoreType.DMA((4,)),),
        after=(first,),
        limit=2,
    )
    passing = trim(HEAD, ring1, (prep, opposite))
    ring2 = [up(passing[0]), down(passing[1])]
    keys = lambda blocks, after=(): call(
        keys_body,
        fast((len(blocks) * COLS, 2 * WIDTH), BF),
        *near(blocks),
        (kv_w, VMEM),
        after=after,
    )
    conv_rims = lambda start, blocks, after=(): call(
        functools.partial(rims_body, start),
        fast(full, F32),
        (place, SCALARS),
        *[(one, VMEM) for one in blocks],
        (conv_w, VMEM),
        after=after,
    )
    rims = conv_rims(HEAD, ring1, (passing[0],))
    near_keys = keys(ring1, (rims,))
    ring2 = later(ring2, (near_keys,))
    ring3 = [up(ring2[0]), down(ring2[1])]
    mid_keys = keys(ring2, (ring2[0],))
    ring3 = later(ring3, (mid_keys,))
    ring4 = [up(ring3[0])]
    far_keys = keys(ring3, (ring3[0],))
    conv_in, hidden, attn_in, query = call(
        level_body,
        (fast(full, BF), fast(full, F32), fast(full, BF), fast(full, BF)),
        (state, VMEM),
        (rims, VMEM),
        (prep, VMEM),
        (conv_w, VMEM),
        (q_w, VMEM),
        *[(one, VMEM) for one in [first, *ring1, *ring2, *ring3, opposite]],
    )
    ring1 = [up(attn_in), down(attn_in)]
    attend_to = lambda weights, early, late: call(
        functools.partial(attend_body, len(early), len(late)),
        fast(full, BF),
        (query, VMEM),
        (hidden, VMEM),
        *early,
        (attn_in, VMEM),
        *near(late),
        *[(w, VMEM) for w in weights],
        scratch=(pltpu.VMEM(((1 + len(late)) * COLS, 2 * WIDTH), BF), pltpu.VMEM(full, BF)),
        micros=4.0,
    )
    early = [(one, VMEM) for one in (near_keys, mid_keys, far_keys)]
    eps = attend_to((kv_w, out_w), early, ring4)
    exchange = lambda x: lax.ppermute(x, "cfg", [(0, 1), (1, 0)])
    other = exchange(eps)
    block = fast((2 * COLS, WIDTH), BF)
    joined = call(
        join_body, (block, block), (conv_in, VMEM), *[(one, VMEM) for one in ring1], after=(eps,)
    )
    ring2 = [up(joined[0]), down(joined[1])]
    near_keys = keys(ring1, (joined[0],))
    state, stats = call(
        functools.partial(update_body, 0),
        (fast(whole, F32), stats_shape),
        (place, SCALARS),
        (prep, VMEM),
        (state, VMEM),
        (eps, VMEM),
        (other, VMEM),
        after=(near_keys,),
    )
    block = fast((HEAD, WIDTH), BF)
    packed = call(
        pack_body, (block, block), (stats, VMEM), *[(one, VMEM) for one in ring2], after=(state,)
    )
    ring3 = [up(packed[0]), down(packed[1])]
    rims = conv_rims(COLS, ring2, (packed[0],))
    mid_keys = keys(ring2, (rims,))
    three, two = call(
        partial_body,
        (stats_shape, stats_shape),
        (stats, VMEM),
        *[(one, VMEM) for one in ring3],
        after=(mid_keys,),
    )
    before, behind = shift(three, 3), shift(two, -3)
    ring3 = later(ring3, (three,))
    ring4 = [up(ring3[0])]
    far_keys = keys(ring3, (ring3[0],))
    attn_in, hidden, query = call(
        second_body,
        (fast(full, BF), fast(full, F32), fast(full, BF)),
        (three, VMEM),
        (before, VMEM),
        (behind, VMEM),
        (state, VMEM),
        (rims, VMEM),
        (prep, VMEM),
        (conv_w, VMEM),
        (q_w, VMEM),
    )
    early = [(one, VMEM) for one in (near_keys, mid_keys, far_keys)]
    eps = attend_to((kv_w, out_w), early, ring4)
    other = exchange(eps)
    return call(
        functools.partial(update_body, 1),
        (shape(whole, F32), shape(whole, F32)),
        (place, SCALARS),
        (prep, VMEM),
        (state, VMEM),
        (eps, VMEM),
        (other, VMEM),
    )


def solution(mesh):
    placed = (
        P(("batch", "patch"), None, None),
        P("cfg", ("batch", "patch"), None, None),
        P("cfg", ("batch", "patch"), None, None),
        P(("batch", "cfg"), None),
        P(),
        P(),
        P(),
        P(),
        P(),
        P(),
        P(),
        P(),
    )
    return jax.shard_map(
        shards,
        mesh=mesh,
        in_specs=placed,
        out_specs=(P(("batch", "patch"), None, None), P(("batch", "patch"), None, None)),
        check_vma=False,
    )
```

```python
import functools
import math

import jax
import jax.numpy as jnp
import numpy as np
from jax import lax
from jax.experimental import pallas as pl
from jax.experimental.pallas import tpu as pltpu
from jax.sharding import PartitionSpec as P

HEADS = 10
GROUPS = 32
STEPS = 2
PATCHES = 8
COLS = 128
WIDTH = 640
PAIRS = HEADS // 2
PER_GROUP = WIDTH // GROUPS
BYTES_PER_MICRO = 3.4e6
BF = jnp.bfloat16
F32 = jnp.float32


def alpha_table():
    start, stop = np.float32(0.00085**0.5), np.float32(0.012**0.5)
    betas = np.linspace(start, stop, 1000, dtype=np.float32) ** 2
    return np.cumprod(1.0 - betas.astype(np.float64)).astype(np.float32)


def dot(a, b):
    return jnp.dot(a, b, preferred_element_type=F32)


def dot_exact(a, b):
    high = a.astype(BF)
    rest = a - high.astype(F32)
    mid = rest.astype(BF)
    low = (rest - mid.astype(F32)).astype(BF)
    return dot(high, b) + (dot(mid, b) + dot(low, b))


HBM, FAR, VMEM, SCALARS = "hbm", "far", "vmem", "scalars"


class Arriving:
    def __init__(self, source, target, sem):
        self.copy = pltpu.make_async_copy(source, target, sem)
        self.target, self.waiting, self.shape = target, True, target.shape
        self.copy.start()

    def wait(self):
        if self.waiting:
            self.copy.wait()
            self.waiting = False

    def __getitem__(self, index):
        self.wait()
        return self.target[index]


def call(body, outs, *args, scratch=(), after=(), micros=0.1, limit=12):
    args += tuple((one, "token") for one in after)
    count, far = len(args), [i for i, (_, where) in enumerate(args) if where == HBM]
    leaves, tree = jax.tree.flatten(outs)
    specs = {
        HBM: pl.BlockSpec(memory_space=pl.ANY),
        FAR: pl.BlockSpec(memory_space=pl.ANY),
        "token": pl.BlockSpec(memory_space=pl.ANY),
        VMEM: pl.BlockSpec(memory_space=pltpu.VMEM),
        SCALARS: pl.BlockSpec(memory_space=pltpu.SMEM),
    }
    buffers = [pltpu.VMEM(args[i][0].shape, args[i][0].dtype) for i in far]
    if far:
        buffers.append(pltpu.SemaphoreType.DMA((len(far),)))

    def wrapped(*refs):
        ins, rest = list(refs[:count]), list(refs[count:])
        if far:
            held, sem = rest[-len(buffers) : -1], rest[-1]
            rest = rest[: -len(buffers)]
            for k, i in enumerate(far):
                ins[i] = Arriving(ins[i], held[k], sem.at[k])
        body(*ins[: count - len(after)], *rest)
        for i in far:
            ins[i].wait()

    def put(arg, where):
        if where not in (VMEM, HBM, FAR):
            return arg
        return pltpu.with_memory_space_constraint(arg, pltpu.VMEM if where == VMEM else pltpu.HBM)

    return pl.pallas_call(
        wrapped,
        out_shape=jax.tree.unflatten(tree, leaves),
        in_specs=[specs[where] for _, where in args],
        out_specs=jax.tree.unflatten(tree, [specs[VMEM] for _ in leaves]),
        scratch_shapes=list(scratch) + buffers,
        compiler_params=pltpu.CompilerParams(vmem_limit_bytes=limit * 2**20),
        cost_estimate=pl.CostEstimate(
            flops=0, bytes_accessed=int(micros * BYTES_PER_MICRO), transcendentals=0
        ),
    )(*[put(arg, where) for arg, where in args])


def fast(dims, dtype):
    return pltpu.VMEM(dims, dtype)


def later(arrays, after):
    count = len(arrays)
    spec = pl.BlockSpec(memory_space=pl.ANY)
    return list(pl.pallas_call(
        lambda *refs: None,
        out_shape=[shape(one.shape, one.dtype) for one in arrays],
        in_specs=[spec] * (count + len(after)),
        out_specs=[spec] * count,
        input_output_aliases={i: i for i in range(count)},
        cost_estimate=pl.CostEstimate(flops=0, bytes_accessed=0, transcendentals=0),
        compiler_params=pltpu.CompilerParams(vmem_limit_bytes=2**20),
    )(*arrays, *after))


def shape(dims, dtype):
    return jax.ShapeDtypeStruct(dims, dtype)


def group_matrix():
    channel = lax.broadcasted_iota(jnp.int32, (WIDTH, 128), 0)
    group = lax.broadcasted_iota(jnp.int32, (WIDTH, 128), 1)
    inside = (channel >= group * PER_GROUP) & (channel < (group + 1) * PER_GROUP)
    return jnp.where(inside, 1.0, 0.0).astype(BF)


def spread_matrix():
    group = lax.broadcasted_iota(jnp.int32, (128, WIDTH), 0)
    channel = lax.broadcasted_iota(jnp.int32, (128, WIDTH), 1)
    inside = (channel >= group * PER_GROUP) & (channel < (group + 1) * PER_GROUP)
    return jnp.where(inside, 1.0, 0.0).astype(BF)


def local_stats(x):
    gather, spread = group_matrix(), spread_matrix()
    mean_c = jnp.mean(x, axis=0, keepdims=True)
    centered = x - mean_c
    dev_c = jnp.sum(centered * centered, axis=0, keepdims=True)
    wide = lambda row: jnp.broadcast_to(row, (8, row.shape[1]))
    mean_g = dot_exact(wide(mean_c), gather) * (1.0 / PER_GROUP)
    off = wide(mean_c) - dot_exact(mean_g, spread)
    dev_g = dot_exact(wide(dev_c) + COLS * (off * off), gather)
    return jnp.concatenate([mean_g[:1], dev_g[:1]], axis=0)


def load_body(*refs):
    count = (len(refs) - 8) // 2
    sources, small, out_ref = refs[:count], refs[count : count + 6], refs[count + 6]
    targets, sem = refs[count + 7 : -1], refs[-1]
    copies = [
        pltpu.make_async_copy(source, target, sem.at[k])
        for k, (source, target) in enumerate(zip(sources, targets))
    ]
    for copy in copies:
        copy.start()
    prep_body(*small, out_ref)
    for copy in copies:
        copy.wait()


def prep_body(steps_ref, table_ref, scale_ref, embed_ref, gn_ref, ln_ref, out_ref):
    half = WIDTH // 2
    lane = lax.broadcasted_iota(jnp.int32, (1, WIDTH), 1)
    low = lane < half
    index = jnp.where(low, lane, lane - half).astype(F32)
    freqs = jnp.exp(index * (-math.log(10000.0) / half))
    table = table_ref[...]
    places = lax.broadcasted_iota(jnp.int32, table.shape, 0) * 128 + lax.broadcasted_iota(
        jnp.int32, table.shape, 1
    )
    pick = lambda t: jnp.sum(jnp.where(places == t, table, 0.0), keepdims=True)
    steps = [steps_ref[0:1, s : s + 1] for s in range(STEPS + 1)]
    levels = [pick(t) for t in steps]
    row = lambda value: jnp.broadcast_to(value, (1, WIDTH))
    rows = []
    for s in range(STEPS):
        angles = steps[s].astype(F32) * freqs
        wave = jnp.where(low, jnp.cos(angles), jnp.sin(angles))
        rows.append(scale_ref[...].reshape(1, WIDTH) * wave + embed_ref[...])
    rows = [r * jax.nn.sigmoid(r) for r in rows]
    for s in range(STEPS):
        now, after = levels[s], levels[s + 1]
        rows.append(row(jnp.sqrt(after / now)))
        rows.append(
            row(jnp.sqrt(1.0 - after) - jnp.sqrt(after) * jnp.sqrt(1.0 - now) / jnp.sqrt(now))
        )
    rows.append(gn_ref[...].reshape(1, WIDTH))
    rows.append(ln_ref[...].reshape(1, WIDTH))
    for r, value in enumerate(rows):
        out_ref[r : r + 1] = value


GN_ROW, LN_ROW = 3 * STEPS, 3 * STEPS + 1
EXTRA = 16
HEAD = COLS + EXTRA
PAD = 32


def stats_rows(stats):
    parts = []
    for _ in range(3):
        part = stats.astype(BF).astype(F32)
        parts.append(part)
        stats = stats - part
    rows = jnp.concatenate(parts + [jnp.zeros((EXTRA - 6, 128), F32)], axis=0)
    return jnp.concatenate([rows, jnp.zeros((EXTRA, WIDTH - 128), F32)], axis=1).astype(BF)


def stats_of(block_ref):
    rows = block_ref[COLS:HEAD, :128].astype(F32)
    return rows[0:2] + rows[2:4] + rows[4:6]


def merge(one, other):
    (count_a, mean_a, dev_a), (count_b, mean_b, dev_b) = one, other
    count, off = count_a + count_b, mean_b - mean_a
    scale = COLS * PER_GROUP * count_a * count_b / count
    return count, mean_a + off * (count_b / count), dev_a + dev_b + scale * (off * off)


def patches(count, stats):
    return count, stats[0:1], stats[1:2]


def first_body(x_ref, attn_ref, conv_ref, block_ref, state_ref, stats_ref, sem):
    places = ((attn_ref, 0), (conv_ref, HEAD))
    copies = [
        pltpu.make_async_copy(source, block_ref.at[pl.ds(start, COLS)], sem.at[k])
        for k, (source, start) in enumerate(places)
    ]
    for copy in copies:
        copy.start()
    x = x_ref[...]
    state_ref[...] = x
    stats = local_stats(x[0])
    stats_ref[0:2] = stats
    block_ref[COLS:HEAD] = stats_rows(stats)
    for copy in copies:
        copy.wait()


def pack_body(stats_ref, up_ref, down_ref, up_block_ref, down_block_ref):
    rows = stats_rows(stats_ref[0:2])
    for source, target in ((up_ref, up_block_ref), (down_ref, down_block_ref)):
        target[:COLS] = source[:COLS]
        target[COLS:] = rows


def partial_body(mine_ref, up_ref, down_ref, three_ref, two_ref):
    two = merge(patches(1, stats_of(up_ref)), patches(1, mine_ref[0:2]))
    three = merge(two, patches(1, stats_of(down_ref)))
    for (_, mean, dev), target in ((three, three_ref), (two, two_ref)):
        target[0:1], target[1:2] = mean, dev


def trim_body(rows, *refs):
    count = len(refs) // 2
    for source, target in zip(refs[:count], refs[count:]):
        target[...] = source[:rows]


def shifted(x):
    place = lax.broadcasted_iota(jnp.int32, x.shape, 0)
    before = jnp.where(place == 0, 0.0, pltpu.roll(x, 1, 0))
    after = jnp.where(place == COLS - 1, 0.0, pltpu.roll(x, COLS - 1, 0))
    return before, after


def conv_row(x, taps):
    before, after = shifted(x)
    return (
        dot(x.astype(BF), taps[1][...])
        + dot(before.astype(BF), taps[0][...])
        + dot(after.astype(BF), taps[2][...])
    )


def rims_body(start, place_ref, up_ref, down_ref, w_ref, out_ref):
    above = up_ref[start : start + COLS].astype(F32) * place_ref[0]
    below = down_ref[start : start + COLS].astype(F32) * place_ref[1]
    out_ref[...] = conv_row(above, [w_ref[0, t] for t in range(3)]) + conv_row(
        below, [w_ref[2, t] for t in range(3)]
    )


def level(step, moments, x, rims, prep_ref, taps, q_w):
    _, mean, dev = moments
    scale = 1.0 / jnp.sqrt(dev * (1.0 / (PATCHES * COLS * PER_GROUP)) + 1e-05)
    rows = jnp.concatenate([jnp.broadcast_to(mean, (8, 128)), jnp.broadcast_to(scale, (8, 128))], axis=0)
    wide = dot_exact(rows, spread_matrix())
    x = x[0]
    normed = (x - wide[0:1]) * (wide[8:9] * prep_ref[GN_ROW : GN_ROW + 1])
    conv_in = normed * jax.nn.sigmoid(normed)
    hidden = x + (conv_row(conv_in, taps) + rims[...]) + prep_ref[step : step + 1]
    mid = jnp.mean(hidden, axis=1, keepdims=True)
    centered = hidden - mid
    var = jnp.mean(centered * centered, axis=1, keepdims=True)
    attn_in = (centered * (1.0 / jnp.sqrt(var + 1e-05)) * prep_ref[LN_ROW : LN_ROW + 1]).astype(BF)
    scale = (WIDTH // HEADS) ** (-0.5) * math.log2(math.e)
    query = (dot(attn_in, q_w[...]) * scale).astype(BF)
    return conv_in.astype(BF), hidden, attn_in, query


def level_body(x_ref, rims_ref, prep_ref, w_ref, q_ref, *refs):
    opposite_ref, conv_in_ref, h_ref, attn_in_ref, query_ref = refs[PATCHES - 1 :]
    total = patches(1, opposite_ref[0:2])
    for ref in refs[: PATCHES - 1]:
        total = merge(total, patches(1, stats_of(ref)))
    taps = [w_ref.at[1, t] for t in range(3)]
    conv_in_ref[:COLS], h_ref[...], attn_in_ref[...], query_ref[...] = level(
        0, total, x_ref[...], rims_ref, prep_ref, taps, q_ref
    )
    conv_in_ref[COLS:] = jnp.zeros((PAD, WIDTH), BF)


def keys_of(rows, kv_ref, out_ref):
    out_ref[...] = dot(jnp.concatenate([ref[:COLS] for ref in rows], axis=0), kv_ref[...]).astype(BF)


def keys_body(*refs):
    keys_of(refs[:-2], *refs[-2:])


def pair_scores(query_ref, parts, pair):
    first_half = lax.broadcasted_iota(jnp.int32, (COLS, 128), 1) < WIDTH // HEADS
    lanes = slice(pair * 128, (pair + 1) * 128)
    query = query_ref[:, lanes]
    zero = jnp.zeros_like(query)
    stacked = jnp.concatenate(
        [jnp.where(first_half, query, zero), jnp.where(first_half, zero, query)], axis=0
    )
    return [
        lax.dot_general(stacked, ref[:, lanes], (((1,), (1,)), ((), ())), preferred_element_type=F32)
        for ref in parts
    ]


def attend(query_ref, parts, mixed_ref):
    first_half = lax.broadcasted_iota(jnp.int32, (COLS, 128), 1) < WIDTH // HEADS
    following = pair_scores(query_ref, parts, 0)
    for pair in range(PAIRS):
        lanes = slice(pair * 128, (pair + 1) * 128)
        values = slice(WIDTH + pair * 128, WIDTH + (pair + 1) * 128)
        scores = following
        if pair + 1 < PAIRS:
            following = pair_scores(query_ref, parts, pair + 1)
        top = functools.reduce(jnp.maximum, [jnp.max(s, axis=1, keepdims=True) for s in scores])
        weights = [jnp.exp2(s - top) for s in scores]
        total = sum(jnp.sum(w, axis=1, keepdims=True) for w in weights)
        product = sum(dot(w.astype(BF), ref[:, values]) for w, ref in zip(weights, parts))
        product = product * (1.0 / total)
        mixed_ref[:, lanes] = jnp.where(first_half, product[:COLS], product[COLS:]).astype(BF)


def attend_body(early, late, query_ref, h_ref, *refs):
    parts, rows = refs[:early], refs[early : early + 1 + late]
    kv_ref, out_w_ref, eps_ref, late_ref, mixed_ref = refs[early + 1 + late :]
    keys_of(rows, kv_ref, late_ref)
    attend(query_ref, (*parts, late_ref), mixed_ref)
    eps_ref[...] = (h_ref[...] + dot(mixed_ref[...], out_w_ref[...])).astype(eps_ref.dtype)


def second_body(
    three_ref, before_ref, after_ref, x_ref, rims_ref, prep_ref, w_ref, q_ref, *refs
):
    attn_in_ref, h_ref, query_ref = refs
    total = merge(patches(3, three_ref[0:2]), patches(2, after_ref[0:2]))
    total = merge(total, patches(3, before_ref[0:2]))
    taps = [w_ref.at[1, t] for t in range(3)]
    _, h_ref[...], attn_in_ref[...], query_ref[...] = level(
        1, total, x_ref[...], rims_ref, prep_ref, taps, q_ref
    )


def guide(place_ref, own_ref, other_ref):
    own, other = own_ref[...].astype(F32), other_ref[...].astype(F32)
    first = place_ref[2] == 0.0
    uncond = jnp.where(first, own, other)
    cond = jnp.where(first, other, own)
    return uncond + 3.0 * (cond - uncond)


def update_body(step, place_ref, prep_ref, x_ref, own_ref, other_ref, state_ref, *refs):
    guided = guide(place_ref, own_ref, other_ref)
    prep, row = prep_ref[...], STEPS + 2 * step
    state = prep[row : row + 1] * x_ref[0] + prep[row + 1 : row + 2] * guided
    state_ref[0] = state
    if step + 1 < STEPS:
        refs[0][0:2] = local_stats(state)
    else:
        refs[0][0] = guided


def shards(
    latent,
    stale_conv,
    stale_attn,
    cond_embed,
    timesteps,
    gn_gain,
    ln_gain,
    time_scale,
    conv_weight,
    q_weight,
    kv_weight,
    out_weight,
):
    patch, branch = lax.axis_index("patch"), lax.axis_index("cfg")
    place = jnp.stack([patch > 0, patch < PATCHES - 1, branch > 0]).astype(F32)
    upward = [(i, (i + 1) % PATCHES) for i in range(PATCHES)]
    downward = [(target, source) for source, target in upward]
    up = lambda x: lax.ppermute(x, "patch", upward)
    down = lambda x: lax.ppermute(x, "patch", downward)
    full = (COLS, WIDTH)
    whole = (1,) + full
    stats_shape = fast((8, 128), F32)
    shift = lambda x, far: lax.ppermute(
        x, "patch", [(i, (i + far) % PATCHES) for i in range(PATCHES)]
    )

    first, state, opposite = call(
        first_body,
        (fast((HEAD + COLS, WIDTH), BF), fast(whole, F32), fast((8, 128), F32)),
        (latent, HBM),
        (stale_attn.reshape(full), FAR),
        (stale_conv.reshape(full), FAR),
        scratch=(pltpu.SemaphoreType.DMA((2,)),),
        after=(place,),
    )
    table = np.ones((8, 128), np.float32)
    table.reshape(-1)[:1000] = alpha_table()
    weights = (conv_weight, q_weight, kv_weight, out_weight)
    trim = lambda rows, blocks, after=(): call(
        functools.partial(trim_body, rows),
        tuple(fast((rows, WIDTH), BF) for _ in blocks),
        *[(one, VMEM) for one in blocks],
        after=after,
    )

    ring1 = [up(first), down(first)]
    opposite = shift(opposite, PATCHES // 2)
    prep, conv_w, q_w, kv_w, out_w = call(
        load_body,
        (fast((8, WIDTH), F32),) + tuple(fast(w.shape, w.dtype) for w in weights),
        *[(w, FAR) for w in weights],
        (timesteps.reshape(1, -1), HBM),
        (jnp.asarray(table), HBM),
        (time_scale, HBM),
        (cond_embed, HBM),
        (gn_gain, HBM),
        (ln_gain, HBM),
        scratch=(pltpu.SemaphoreType.DMA((4,)),),
        after=(first,),
        limit=2,
    )
    passing = trim(HEAD, ring1, (prep, opposite))
    ring2 = [up(passing[0]), down(passing[1])]
    keys = lambda blocks, after=(): call(
        keys_body,
        fast((len(blocks) * COLS, 2 * WIDTH), BF),
        *[(one, VMEM) for one in blocks],
        (kv_w, VMEM),
        after=after,
    )
    conv_rims = lambda start, blocks, after=(): call(
        functools.partial(rims_body, start),
        fast(full, F32),
        (place, SCALARS),
        *[(one, VMEM) for one in blocks],
        (conv_w, VMEM),
        after=after,
    )
    rims = conv_rims(HEAD, ring1, (passing[0],))
    near_keys = keys(ring1, (rims,))
    ring2 = later(ring2, (near_keys,))
    ring3 = [up(ring2[0]), down(ring2[1])]
    mid_keys = keys(ring2, (ring2[0],))
    ring3 = later(ring3, (mid_keys,))
    ring4 = [up(ring3[0])]
    far_keys = keys(ring3, (ring3[0],))
    conv_in, hidden, attn_in, query = call(
        level_body,
        (fast((COLS + PAD, WIDTH), BF), fast(full, F32), fast(full, BF), fast(full, BF)),
        (state, VMEM),
        (rims, VMEM),
        (prep, VMEM),
        (conv_w, VMEM),
        (q_w, VMEM),
        *[(one, VMEM) for one in [first, *ring1, *ring2, *ring3, opposite]],
    )
    ring1 = [up(attn_in), down(attn_in)]
    attend_to = lambda weights, early, late: call(
        functools.partial(attend_body, len(early), len(late)),
        fast(full, BF),
        (query, VMEM),
        (hidden, VMEM),
        *early,
        (attn_in, VMEM),
        *[(one, VMEM) for one in late],
        *[(w, VMEM) for w in weights],
        scratch=(pltpu.VMEM(((1 + len(late)) * COLS, 2 * WIDTH), BF), pltpu.VMEM(full, BF)),
        limit=20,
    )
    early = [(one, VMEM) for one in (near_keys, mid_keys, far_keys)]
    eps = attend_to((kv_w, out_w), early, ring4)
    exchange = lambda x: lax.ppermute(x, "cfg", [(0, 1), (1, 0)])
    other = exchange(eps)
    ring1 = later(ring1, (eps,))
    ring2 = [up(ring1[0]), down(ring1[1])]
    near_keys = keys(ring1, (eps,))
    (conv_in,) = later([conv_in], (near_keys,))
    rims_in = [up(conv_in), down(conv_in)]
    state, stats = call(
        functools.partial(update_body, 0),
        (fast(whole, F32), stats_shape),
        (place, SCALARS),
        (prep, VMEM),
        (state, VMEM),
        (eps, VMEM),
        (other, VMEM),
        after=(near_keys,),
    )
    block = fast((HEAD, WIDTH), BF)
    packed = call(
        pack_body, (block, block), (stats, VMEM), *[(one, VMEM) for one in ring2], after=(state,)
    )
    ring3 = [up(packed[0]), down(packed[1])]
    rims = conv_rims(0, rims_in, (packed[0],))
    mid_keys = keys(ring2, (rims,))
    three, two = call(
        partial_body,
        (stats_shape, stats_shape),
        (stats, VMEM),
        *[(one, VMEM) for one in ring3],
        after=(mid_keys,),
    )
    before, behind = shift(three, 3), shift(two, -3)
    ring3 = later(ring3, (three,))
    ring4 = [up(ring3[0])]
    far_keys = keys(ring3, (ring3[0],))
    attn_in, hidden, query = call(
        second_body,
        (fast(full, BF), fast(full, F32), fast(full, BF)),
        (three, VMEM),
        (before, VMEM),
        (behind, VMEM),
        (state, VMEM),
        (rims, VMEM),
        (prep, VMEM),
        (conv_w, VMEM),
        (q_w, VMEM),
    )
    early = [(one, VMEM) for one in (near_keys, mid_keys, far_keys)]
    eps = attend_to((kv_w, out_w), early, ring4)
    other = exchange(eps)
    return call(
        functools.partial(update_body, 1),
        (shape(whole, F32), shape(whole, F32)),
        (place, SCALARS),
        (prep, VMEM),
        (state, VMEM),
        (eps, VMEM),
        (other, VMEM),
    )


def solution(mesh):
    placed = (
        P(("batch", "patch"), None, None),
        P("cfg", ("batch", "patch"), None, None),
        P("cfg", ("batch", "patch"), None, None),
        P(("batch", "cfg"), None),
        P(),
        P(),
        P(),
        P(),
        P(),
        P(),
        P(),
        P(),
    )
    return jax.shard_map(
        shards,
        mesh=mesh,
        in_specs=placed,
        out_specs=(P(("batch", "patch"), None, None), P(("batch", "patch"), None, None)),
        check_vma=False,
    )
```

```python
import functools
import math

import jax
import jax.numpy as jnp
import numpy as np
from jax import lax
from jax.experimental import pallas as pl
from jax.experimental.pallas import tpu as pltpu
from jax.sharding import PartitionSpec as P

HEADS = 10
GROUPS = 32
STEPS = 2
PATCHES = 8
COLS = 128
WIDTH = 640
PAIRS = HEADS // 2
PER_GROUP = WIDTH // GROUPS
BF = jnp.bfloat16
F32 = jnp.float32


def alpha_table():
    start, stop = np.float32(0.00085**0.5), np.float32(0.012**0.5)
    betas = np.linspace(start, stop, 1000, dtype=np.float32) ** 2
    return np.cumprod(1.0 - betas.astype(np.float64)).astype(np.float32)


def dot(a, b):
    return jnp.dot(a, b, preferred_element_type=F32)


def dot_exact(a, b):
    rows = a.shape[0]
    high = a.astype(BF).astype(F32)
    mid = (a - high).astype(BF).astype(F32)
    product = dot(jnp.concatenate([high, mid, (a - high) - mid], axis=0).astype(BF), b)
    return product[:rows] + (product[rows : 2 * rows] + product[2 * rows :])


HBM, FAR, VMEM, SCALARS = "hbm", "far", "vmem", "scalars"


class Arriving:
    def __init__(self, source, target, sem):
        self.copy = pltpu.make_async_copy(source, target, sem)
        self.target, self.waiting, self.shape = target, True, target.shape
        self.copy.start()

    def wait(self):
        if self.waiting:
            self.copy.wait()
            self.waiting = False

    def __getitem__(self, index):
        self.wait()
        return self.target[index]


def call(body, outs, *args, scratch=(), after=(), outs_far=False, limit=12):
    args += tuple((one, "token") for one in after)
    count, far = len(args), [i for i, (_, where) in enumerate(args) if where == HBM]
    leaves, tree = jax.tree.flatten(outs)
    specs = {
        HBM: pl.BlockSpec(memory_space=pl.ANY),
        FAR: pl.BlockSpec(memory_space=pl.ANY),
        "token": pl.BlockSpec(memory_space=pl.ANY),
        VMEM: pl.BlockSpec(memory_space=pltpu.VMEM),
        SCALARS: pl.BlockSpec(memory_space=pltpu.SMEM),
    }
    buffers = [pltpu.VMEM(args[i][0].shape, args[i][0].dtype) for i in far]
    if far:
        buffers.append(pltpu.SemaphoreType.DMA((len(far),)))

    def wrapped(*refs):
        ins, rest = list(refs[:count]), list(refs[count:])
        if far:
            held, sem = rest[-len(buffers) : -1], rest[-1]
            rest = rest[: -len(buffers)]
            for k, i in enumerate(far):
                ins[i] = Arriving(ins[i], held[k], sem.at[k])
        body(*ins[: count - len(after)], *rest)
        for i in far:
            ins[i].wait()

    def put(arg, where):
        if where not in (VMEM, HBM, FAR):
            return arg
        return pltpu.with_memory_space_constraint(arg, pltpu.VMEM if where == VMEM else pltpu.HBM)

    return pl.pallas_call(
        wrapped,
        out_shape=jax.tree.unflatten(tree, leaves),
        in_specs=[specs[where] for _, where in args],
        out_specs=jax.tree.unflatten(tree, [specs[FAR if outs_far else VMEM] for _ in leaves]),
        scratch_shapes=list(scratch) + buffers,
        compiler_params=pltpu.CompilerParams(vmem_limit_bytes=limit * 2**20),
    )(*[put(arg, where) for arg, where in args])


def fast(dims, dtype):
    return pltpu.VMEM(dims, dtype)


def later(arrays, after):
    count = len(arrays)
    spec = pl.BlockSpec(memory_space=pl.ANY)
    return list(pl.pallas_call(
        lambda *refs: None,
        out_shape=[shape(one.shape, one.dtype) for one in arrays],
        in_specs=[spec] * (count + len(after)),
        out_specs=[spec] * count,
        input_output_aliases={i: i for i in range(count)},
        cost_estimate=pl.CostEstimate(flops=0, bytes_accessed=0, transcendentals=0),
        compiler_params=pltpu.CompilerParams(vmem_limit_bytes=2**20),
    )(*arrays, *after))


def shape(dims, dtype):
    return jax.ShapeDtypeStruct(dims, dtype)


def group_matrix():
    channel = lax.broadcasted_iota(jnp.int32, (WIDTH, 128), 0)
    group = lax.broadcasted_iota(jnp.int32, (WIDTH, 128), 1)
    inside = (channel >= group * PER_GROUP) & (channel < (group + 1) * PER_GROUP)
    return jnp.where(inside, 1.0, 0.0).astype(BF)


def spread_matrix():
    group = lax.broadcasted_iota(jnp.int32, (128, WIDTH), 0)
    channel = lax.broadcasted_iota(jnp.int32, (128, WIDTH), 1)
    inside = (channel >= group * PER_GROUP) & (channel < (group + 1) * PER_GROUP)
    return jnp.where(inside, 1.0, 0.0).astype(BF)


def local_stats(x):
    gather, spread = group_matrix(), spread_matrix()
    mean_c = jnp.mean(x, axis=0, keepdims=True)
    centered = x - mean_c
    dev_c = jnp.sum(centered * centered, axis=0, keepdims=True)
    wide = lambda row: jnp.broadcast_to(row, (8, row.shape[1]))
    mean_g = dot_exact(wide(mean_c), gather) * (1.0 / PER_GROUP)
    off = wide(mean_c) - dot_exact(mean_g, spread)
    dev_g = dot_exact(wide(dev_c) + COLS * (off * off), gather)
    return jnp.concatenate([mean_g[:1], dev_g[:1]], axis=0)


def load_body(*refs):
    count = (len(refs) - 8) // 2
    sources, small, out_ref = refs[:count], refs[count : count + 6], refs[count + 6]
    targets, sem = refs[count + 7 : -1], refs[-1]
    copies = [
        pltpu.make_async_copy(source, target, sem.at[k])
        for k, (source, target) in enumerate(zip(sources, targets))
    ]
    for copy in copies:
        copy.start()
    prep_body(*small, out_ref)
    for copy in copies:
        copy.wait()


def prep_body(steps_ref, table_ref, scale_ref, embed_ref, gn_ref, ln_ref, out_ref):
    half = WIDTH // 2
    lane = lax.broadcasted_iota(jnp.int32, (1, WIDTH), 1)
    low = lane < half
    index = jnp.where(low, lane, lane - half).astype(F32)
    freqs = jnp.exp(index * (-math.log(10000.0) / half))
    table = table_ref[...]
    places = lax.broadcasted_iota(jnp.int32, table.shape, 0) * 128 + lax.broadcasted_iota(
        jnp.int32, table.shape, 1
    )
    pick = lambda t: jnp.sum(jnp.where(places == t, table, 0.0), keepdims=True)
    steps = [steps_ref[0:1, s : s + 1] for s in range(STEPS + 1)]
    levels = [pick(t) for t in steps]
    row = lambda value: jnp.broadcast_to(value, (1, WIDTH))
    rows = []
    for s in range(STEPS):
        angles = steps[s].astype(F32) * freqs
        wave = jnp.where(low, jnp.cos(angles), jnp.sin(angles))
        rows.append(scale_ref[...].reshape(1, WIDTH) * wave + embed_ref[...])
    rows = [r * jax.nn.sigmoid(r) for r in rows]
    for s in range(STEPS):
        now, after = levels[s], levels[s + 1]
        rows.append(row(jnp.sqrt(after / now)))
        rows.append(
            row(jnp.sqrt(1.0 - after) - jnp.sqrt(after) * jnp.sqrt(1.0 - now) / jnp.sqrt(now))
        )
    rows.append(gn_ref[...].reshape(1, WIDTH))
    rows.append(ln_ref[...].reshape(1, WIDTH))
    for r, value in enumerate(rows):
        out_ref[r : r + 1] = value


GN_ROW, LN_ROW = 3 * STEPS, 3 * STEPS + 1
EXTRA = 16
HEAD = COLS + EXTRA
PAD = 32
CHUNKS = 4


def stats_rows(stats):
    parts = []
    for _ in range(3):
        part = stats.astype(BF).astype(F32)
        parts.append(part)
        stats = stats - part
    rows = jnp.concatenate(parts + [jnp.zeros((EXTRA - 6, 128), F32)], axis=0)
    return jnp.concatenate([rows, jnp.zeros((EXTRA, WIDTH - 128), F32)], axis=1).astype(BF)


def stats_of(block_ref):
    rows = block_ref[COLS:HEAD, :128].astype(F32)
    return rows[0:2] + rows[2:4] + rows[4:6]


def merge(one, other):
    (count_a, mean_a, dev_a), (count_b, mean_b, dev_b) = one, other
    count, off = count_a + count_b, mean_b - mean_a
    scale = COLS * PER_GROUP * count_a * count_b / count
    return count, mean_a + off * (count_b / count), dev_a + dev_b + scale * (off * off)


def patches(count, stats):
    return count, stats[0:1], stats[1:2]


def first_body(x_ref, attn_ref, conv_ref, block_ref, state_ref, stats_ref, sem):
    places = ((attn_ref, 0), (conv_ref, HEAD))
    copies = [
        pltpu.make_async_copy(source, block_ref.at[pl.ds(start, COLS)], sem.at[k])
        for k, (source, start) in enumerate(places)
    ]
    for copy in copies:
        copy.start()
    x = x_ref[...]
    state_ref[...] = x
    stats = local_stats(x[0])
    stats_ref[0:2] = stats
    block_ref[COLS:HEAD] = stats_rows(stats)
    for copy in copies:
        copy.wait()


def pack_body(stats_ref, up_ref, down_ref, up_block_ref, down_block_ref):
    rows = stats_rows(stats_ref[0:2])
    for source, target in ((up_ref, up_block_ref), (down_ref, down_block_ref)):
        target[:COLS] = source[:COLS]
        target[COLS:] = rows


def partial_body(mine_ref, up_ref, down_ref, three_ref, two_ref):
    two = merge(patches(1, stats_of(up_ref)), patches(1, mine_ref[0:2]))
    three = merge(two, patches(1, stats_of(down_ref)))
    for (_, mean, dev), target in ((three, three_ref), (two, two_ref)):
        target[0:1], target[1:2] = mean, dev


def trim_body(rows, *refs):
    count = len(refs) // 2
    for source, target in zip(refs[:count], refs[count:]):
        target[...] = source[:rows]


def shifted(x):
    place = lax.broadcasted_iota(jnp.int32, x.shape, 0)
    before = jnp.where(place == 0, 0.0, pltpu.roll(x, 1, 0))
    after = jnp.where(place == COLS - 1, 0.0, pltpu.roll(x, COLS - 1, 0))
    return before, after


def conv_row(x, taps):
    before, after = shifted(x)
    return (
        dot(x.astype(BF), taps[1][...])
        + dot(before.astype(BF), taps[0][...])
        + dot(after.astype(BF), taps[2][...])
    )


def rims_body(start, place_ref, up_ref, down_ref, w_ref, out_ref):
    above = up_ref[start : start + COLS].astype(F32) * place_ref[0]
    below = down_ref[start : start + COLS].astype(F32) * place_ref[1]
    out_ref[...] = conv_row(above, [w_ref[0, t] for t in range(3)]) + conv_row(
        below, [w_ref[2, t] for t in range(3)]
    )


def level(step, moments, x, rims, prep_ref, taps, q_w):
    _, mean, dev = moments
    scale = 1.0 / jnp.sqrt(dev * (1.0 / (PATCHES * COLS * PER_GROUP)) + 1e-05)
    first_rows = lax.broadcasted_iota(jnp.int32, (8, 128), 0) < 4
    wide = dot_exact(jnp.where(first_rows, mean, scale), spread_matrix())
    x = x[0]
    normed = (x - wide[0:1]) * (wide[4:5] * prep_ref[GN_ROW : GN_ROW + 1])
    conv_in = normed * jax.nn.sigmoid(normed)
    hidden = x + (conv_row(conv_in, taps) + rims[...]) + prep_ref[step : step + 1]
    mid = jnp.mean(hidden, axis=1, keepdims=True)
    centered = hidden - mid
    var = jnp.mean(centered * centered, axis=1, keepdims=True)
    attn_in = (centered * (1.0 / jnp.sqrt(var + 1e-05)) * prep_ref[LN_ROW : LN_ROW + 1]).astype(BF)
    scale = (WIDTH // HEADS) ** (-0.5) * math.log2(math.e)
    query = (dot(attn_in, q_w[...]) * scale).astype(BF)
    return conv_in.astype(BF), hidden, attn_in, query


def level_body(x_ref, rims_ref, prep_ref, w_ref, q_ref, *refs):
    opposite_ref, conv_in_ref, h_ref, attn_in_ref, query_ref = refs[PATCHES - 1 :]
    total = patches(1, opposite_ref[0:2])
    for ref in refs[: PATCHES - 1]:
        total = merge(total, patches(1, stats_of(ref)))
    taps = [w_ref.at[1, t] for t in range(3)]
    conv_in_ref[:COLS], h_ref[...], attn_in_ref[...], query_ref[...] = level(
        0, total, x_ref[...], rims_ref, prep_ref, taps, q_ref
    )
    conv_in_ref[COLS:] = jnp.zeros((PAD, WIDTH), BF)


def keys_of(rows, kv_ref, out_ref):
    out_ref[...] = dot(jnp.concatenate([ref[:COLS] for ref in rows], axis=0), kv_ref[...]).astype(BF)


def keys_body(*refs):
    keys_of(refs[:-2], *refs[-2:])


def pair_scores(query_ref, parts, pair):
    first_half = lax.broadcasted_iota(jnp.int32, (COLS, 128), 1) < WIDTH // HEADS
    lanes = slice(pair * 128, (pair + 1) * 128)
    query = query_ref[:, lanes]
    zero = jnp.zeros_like(query)
    stacked = jnp.concatenate(
        [jnp.where(first_half, query, zero), jnp.where(first_half, zero, query)], axis=0
    )
    return [
        lax.dot_general(stacked, ref[:, lanes], (((1,), (1,)), ((), ())), preferred_element_type=F32)
        for ref in parts
    ]


def attend(query_ref, parts, mixed_ref):
    first_half = lax.broadcasted_iota(jnp.int32, (COLS, 128), 1) < WIDTH // HEADS
    following = pair_scores(query_ref, parts, 0)
    for pair in range(PAIRS):
        lanes = slice(pair * 128, (pair + 1) * 128)
        values = slice(WIDTH + pair * 128, WIDTH + (pair + 1) * 128)
        scores = following
        if pair + 1 < PAIRS:
            following = pair_scores(query_ref, parts, pair + 1)
        top = functools.reduce(jnp.maximum, [jnp.max(s, axis=1, keepdims=True) for s in scores])
        weights = [jnp.exp2(s - top) for s in scores]
        total = sum(jnp.sum(w, axis=1, keepdims=True) for w in weights)
        product = sum(dot(w.astype(BF), ref[:, values]) for w, ref in zip(weights, parts))
        product = product * (1.0 / total)
        mixed_ref[:, lanes] = jnp.where(first_half, product[:COLS], product[COLS:]).astype(BF)


def attend_body(early, late, ready, query_ref, h_ref, *refs):
    parts, rows, done = refs[:early], refs[early : early + 1 + late], refs[early + 1 + late :][:ready]
    kv_ref, out_w_ref, eps_ref, late_ref, mixed_ref = refs[early + 1 + late + ready :]
    keys_of(rows, kv_ref, late_ref.at[: (1 + late) * COLS])
    for ref in done:
        late_ref[COLS:] = ref[...]
    attend(query_ref, (*parts, late_ref), mixed_ref)
    eps_ref[...] = (h_ref[...] + dot(mixed_ref[...], out_w_ref[...])).astype(eps_ref.dtype)


def second_body(
    three_ref, before_ref, after_ref, x_ref, rims_ref, prep_ref, w_ref, q_ref, *refs
):
    attn_in_ref, h_ref, query_ref = refs
    total = merge(patches(3, three_ref[0:2]), patches(2, after_ref[0:2]))
    total = merge(total, patches(3, before_ref[0:2]))
    taps = [w_ref.at[1, t] for t in range(3)]
    _, h_ref[...], attn_in_ref[...], query_ref[...] = level(
        1, total, x_ref[...], rims_ref, prep_ref, taps, q_ref
    )


def guide(first, own, other):
    uncond = jnp.where(first, own, other)
    cond = jnp.where(first, other, own)
    return uncond + 3.0 * (cond - uncond)


def update_body(place_ref, prep_ref, x_ref, own_ref, other_ref, state_ref, stats_ref):
    own, other = own_ref[...].astype(F32), other_ref[...].astype(F32)
    guided = guide(place_ref[2] == 0.0, own, other)
    state = prep_ref[STEPS : STEPS + 1] * x_ref[0] + prep_ref[STEPS + 1 : STEPS + 2] * guided
    state_ref[0] = state
    stats_ref[0:2] = local_stats(state)


def last_body(
    place_ref, prep_ref, x_ref, own_ref, other_ref, state_ref, guided_ref, state_held, guided_held, sem
):
    row, step = STEPS + 2 * (STEPS - 1), COLS // CHUNKS
    copies = []
    for k in range(CHUNKS):
        part = slice(k * step, (k + 1) * step)
        own, other = own_ref[part].astype(F32), other_ref[part].astype(F32)
        guided = guide(place_ref[2] == 0.0, own, other)
        guided_held[part] = guided
        state_held[part] = prep_ref[row : row + 1] * x_ref[0, part] + prep_ref[row + 1 : row + 2] * guided
        for one, (held, target) in enumerate(((guided_held, guided_ref), (state_held, state_ref))):
            copy = pltpu.make_async_copy(held.at[part], target.at[0, part], sem.at[2 * k + one])
            copy.start()
            copies.append(copy)
    for copy in copies:
        copy.wait()


def shards(
    latent,
    stale_conv,
    stale_attn,
    cond_embed,
    timesteps,
    gn_gain,
    ln_gain,
    time_scale,
    conv_weight,
    q_weight,
    kv_weight,
    out_weight,
):
    patch, branch = lax.axis_index("patch"), lax.axis_index("cfg")
    place = jnp.stack([patch > 0, patch < PATCHES - 1, branch > 0]).astype(F32)
    upward = [(i, (i + 1) % PATCHES) for i in range(PATCHES)]
    downward = [(target, source) for source, target in upward]
    up = lambda x: lax.ppermute(x, "patch", upward)
    down = lambda x: lax.ppermute(x, "patch", downward)
    full = (COLS, WIDTH)
    whole = (1,) + full
    stats_shape = fast((8, 128), F32)
    shift = lambda x, far: lax.ppermute(
        x, "patch", [(i, (i + far) % PATCHES) for i in range(PATCHES)]
    )

    first, state, opposite = call(
        first_body,
        (fast((HEAD + COLS, WIDTH), BF), fast(whole, F32), fast((8, 128), F32)),
        (latent, HBM),
        (stale_attn.reshape(full), FAR),
        (stale_conv.reshape(full), FAR),
        scratch=(pltpu.SemaphoreType.DMA((2,)),),
        after=(place,),
    )
    table = np.ones((8, 128), np.float32)
    table.reshape(-1)[:1000] = alpha_table()
    weights = (conv_weight, q_weight, kv_weight, out_weight)
    trim = lambda rows, blocks, after=(): call(
        functools.partial(trim_body, rows),
        tuple(fast((rows, WIDTH), BF) for _ in blocks),
        *[(one, VMEM) for one in blocks],
        after=after,
    )

    ring1 = [up(first), down(first)]
    opposite = shift(opposite, PATCHES // 2)
    prep, conv_w, q_w, kv_w, out_w = call(
        load_body,
        (fast((8, WIDTH), F32),) + tuple(fast(w.shape, w.dtype) for w in weights),
        *[(w, FAR) for w in weights],
        (timesteps.reshape(1, -1), HBM),
        (jnp.asarray(table), HBM),
        (time_scale, HBM),
        (cond_embed, HBM),
        (gn_gain, HBM),
        (ln_gain, HBM),
        scratch=(pltpu.SemaphoreType.DMA((4,)),),
        after=(first,),
        limit=2,
    )
    passing = trim(HEAD, ring1, (prep, opposite))
    ring2 = [up(passing[0]), down(passing[1])]
    keys = lambda blocks, after=(): call(
        keys_body,
        fast((len(blocks) * COLS, 2 * WIDTH), BF),
        *[(one, VMEM) for one in blocks],
        (kv_w, VMEM),
        after=after,
    )
    conv_rims = lambda start, blocks, after=(): call(
        functools.partial(rims_body, start),
        fast(full, F32),
        (place, SCALARS),
        *[(one, VMEM) for one in blocks],
        (conv_w, VMEM),
        after=after,
    )
    rims = conv_rims(HEAD, ring1, (passing[0],))
    near_keys = keys(ring1, (rims,))
    ring2 = later(ring2, (near_keys,))
    ring3 = [up(ring2[0]), down(ring2[1])]
    mid_keys = keys(ring2, (ring2[0],))
    ring3 = later(ring3, (mid_keys,))
    ring4 = [up(ring3[0])]
    far_keys = keys(ring3, (ring3[0],))
    conv_in, hidden, attn_in, query = call(
        level_body,
        (fast((COLS + PAD, WIDTH), BF), fast(full, F32), fast(full, BF), fast(full, BF)),
        (state, VMEM),
        (rims, VMEM),
        (prep, VMEM),
        (conv_w, VMEM),
        (q_w, VMEM),
        *[(one, VMEM) for one in [first, *ring1, *ring2, *ring3, opposite]],
    )
    ring1 = [up(attn_in), down(attn_in)]
    attend_to = lambda weights, early, late, ready: call(
        functools.partial(attend_body, len(early), len(late), len(ready)),
        fast(full, BF),
        (query, VMEM),
        (hidden, VMEM),
        *early,
        (attn_in, VMEM),
        *[(one, VMEM) for one in late],
        *[(one, VMEM) for one in ready],
        *[(w, VMEM) for w in weights],
        scratch=(pltpu.VMEM((2 * COLS, 2 * WIDTH), BF), pltpu.VMEM(full, BF)),
        limit=20,
    )
    early = [(one, VMEM) for one in (near_keys, mid_keys, far_keys)]
    eps = attend_to((kv_w, out_w), early, ring4, [])
    exchange = lambda x: lax.ppermute(x, "cfg", [(0, 1), (1, 0)])
    other = exchange(eps)
    ring1 = later(ring1, (eps,))
    ring2 = [up(ring1[0]), down(ring1[1])]
    near_keys = keys(ring1, (eps,))
    (conv_in,) = later([conv_in], (near_keys,))
    rims_in = [up(conv_in), down(conv_in)]
    state, stats = call(
        update_body,
        (fast(whole, F32), stats_shape),
        (place, SCALARS),
        (prep, VMEM),
        (state, VMEM),
        (eps, VMEM),
        (other, VMEM),
        after=(near_keys,),
    )
    block = fast((HEAD, WIDTH), BF)
    packed = call(
        pack_body, (block, block), (stats, VMEM), *[(one, VMEM) for one in ring2], after=(state,)
    )
    ring3 = [up(packed[0]), down(packed[1])]
    rims = conv_rims(0, rims_in, (packed[0],))
    mid_keys = keys(ring2, (rims,))
    three, two = call(
        partial_body,
        (stats_shape, stats_shape),
        (stats, VMEM),
        *[(one, VMEM) for one in ring3],
        after=(mid_keys,),
    )
    before, behind = shift(three, 3), shift(two, -3)
    ring3 = later(ring3, (three,))
    ring4 = [up(ring3[0])]
    far_keys = keys(ring3, (ring3[0],))
    last_keys = keys(ring4, (far_keys,))
    attn_in, hidden, query = call(
        second_body,
        (fast(full, BF), fast(full, F32), fast(full, BF)),
        (three, VMEM),
        (before, VMEM),
        (behind, VMEM),
        (state, VMEM),
        (rims, VMEM),
        (prep, VMEM),
        (conv_w, VMEM),
        (q_w, VMEM),
        after=(last_keys,),
    )
    early = [(one, VMEM) for one in (near_keys, mid_keys, far_keys)]
    eps = attend_to((kv_w, out_w), early, [], [last_keys])
    other = exchange(eps)
    return call(
        last_body,
        (shape(whole, F32), shape(whole, F32)),
        (place, SCALARS),
        (prep, VMEM),
        (state, VMEM),
        (eps, VMEM),
        (other, VMEM),
        scratch=(
            pltpu.VMEM(full, F32),
            pltpu.VMEM(full, F32),
            pltpu.SemaphoreType.DMA((2 * CHUNKS,)),
        ),
        outs_far=True,
    )


def solution(mesh):
    placed = (
        P(("batch", "patch"), None, None),
        P("cfg", ("batch", "patch"), None, None),
        P("cfg", ("batch", "patch"), None, None),
        P(("batch", "cfg"), None),
        P(),
        P(),
        P(),
        P(),
        P(),
        P(),
        P(),
        P(),
    )
    return jax.shard_map(
        shards,
        mesh=mesh,
        in_specs=placed,
        out_specs=(P(("batch", "patch"), None, None), P(("batch", "patch"), None, None)),
        check_vma=False,
    )
```

```python
import functools
import math

import jax
import jax.numpy as jnp
import numpy as np
from jax import lax
from jax.experimental import pallas as pl
from jax.experimental.pallas import tpu as pltpu
from jax.sharding import PartitionSpec as P

HEADS = 10
GROUPS = 32
STEPS = 2
PATCHES = 8
COLS = 128
WIDTH = 640
PAIRS = HEADS // 2
PER_GROUP = WIDTH // GROUPS
BF = jnp.bfloat16
F32 = jnp.float32


def alpha_table():
    start, stop = np.float32(0.00085**0.5), np.float32(0.012**0.5)
    betas = np.linspace(start, stop, 1000, dtype=np.float32) ** 2
    return np.cumprod(1.0 - betas.astype(np.float64)).astype(np.float32)


def dot(a, b):
    return jnp.dot(a, b, preferred_element_type=F32)


def dot_exact(a, b):
    rows = a.shape[0]
    high = a.astype(BF).astype(F32)
    mid = (a - high).astype(BF).astype(F32)
    product = dot(jnp.concatenate([high, mid, (a - high) - mid], axis=0).astype(BF), b)
    return product[:rows] + (product[rows : 2 * rows] + product[2 * rows :])


HBM, FAR, VMEM, SCALARS = "hbm", "far", "vmem", "scalars"


class Arriving:
    def __init__(self, source, target, sem):
        self.copy = pltpu.make_async_copy(source, target, sem)
        self.target, self.waiting, self.shape = target, True, target.shape
        self.copy.start()

    def wait(self):
        if self.waiting:
            self.copy.wait()
            self.waiting = False

    def __getitem__(self, index):
        self.wait()
        return self.target[index]


def call(body, outs, *args, scratch=(), after=(), outs_far=False, limit=12):
    args += tuple((one, "token") for one in after)
    count, far = len(args), [i for i, (_, where) in enumerate(args) if where == HBM]
    leaves, tree = jax.tree.flatten(outs)
    specs = {
        HBM: pl.BlockSpec(memory_space=pl.ANY),
        FAR: pl.BlockSpec(memory_space=pl.ANY),
        "token": pl.BlockSpec(memory_space=pl.ANY),
        VMEM: pl.BlockSpec(memory_space=pltpu.VMEM),
        SCALARS: pl.BlockSpec(memory_space=pltpu.SMEM),
    }
    buffers = [pltpu.VMEM(args[i][0].shape, args[i][0].dtype) for i in far]
    if far:
        buffers.append(pltpu.SemaphoreType.DMA((len(far),)))

    def wrapped(*refs):
        ins, rest = list(refs[:count]), list(refs[count:])
        if far:
            held, sem = rest[-len(buffers) : -1], rest[-1]
            rest = rest[: -len(buffers)]
            for k, i in enumerate(far):
                ins[i] = Arriving(ins[i], held[k], sem.at[k])
        body(*ins[: count - len(after)], *rest)
        for i in far:
            ins[i].wait()

    def put(arg, where):
        if where not in (VMEM, HBM, FAR):
            return arg
        return pltpu.with_memory_space_constraint(arg, pltpu.VMEM if where == VMEM else pltpu.HBM)

    return pl.pallas_call(
        wrapped,
        out_shape=jax.tree.unflatten(tree, leaves),
        in_specs=[specs[where] for _, where in args],
        out_specs=jax.tree.unflatten(tree, [specs[FAR if outs_far else VMEM] for _ in leaves]),
        scratch_shapes=list(scratch) + buffers,
        compiler_params=pltpu.CompilerParams(vmem_limit_bytes=limit * 2**20),
    )(*[put(arg, where) for arg, where in args])


def fast(dims, dtype):
    return pltpu.VMEM(dims, dtype)


def later(arrays, after):
    count = len(arrays)
    spec = pl.BlockSpec(memory_space=pl.ANY)
    return list(pl.pallas_call(
        lambda *refs: None,
        out_shape=[shape(one.shape, one.dtype) for one in arrays],
        in_specs=[spec] * (count + len(after)),
        out_specs=[spec] * count,
        input_output_aliases={i: i for i in range(count)},
        cost_estimate=pl.CostEstimate(flops=0, bytes_accessed=0, transcendentals=0),
        compiler_params=pltpu.CompilerParams(vmem_limit_bytes=2**20),
    )(*arrays, *after))


def shape(dims, dtype):
    return jax.ShapeDtypeStruct(dims, dtype)


def group_matrix():
    channel = lax.broadcasted_iota(jnp.int32, (WIDTH, 128), 0)
    group = lax.broadcasted_iota(jnp.int32, (WIDTH, 128), 1)
    inside = (channel >= group * PER_GROUP) & (channel < (group + 1) * PER_GROUP)
    return jnp.where(inside, 1.0, 0.0).astype(BF)


def spread_matrix():
    group = lax.broadcasted_iota(jnp.int32, (128, WIDTH), 0)
    channel = lax.broadcasted_iota(jnp.int32, (128, WIDTH), 1)
    inside = (channel >= group * PER_GROUP) & (channel < (group + 1) * PER_GROUP)
    return jnp.where(inside, 1.0, 0.0).astype(BF)


def local_stats(x):
    gather, spread = group_matrix(), spread_matrix()
    mean_c = jnp.mean(x, axis=0, keepdims=True)
    centered = x - mean_c
    dev_c = jnp.sum(centered * centered, axis=0, keepdims=True)
    wide = lambda row: jnp.broadcast_to(row, (8, row.shape[1]))
    mean_g = dot_exact(wide(mean_c), gather) * (1.0 / PER_GROUP)
    off = wide(mean_c) - dot_exact(mean_g, spread)
    dev_g = dot_exact(wide(dev_c) + COLS * (off * off), gather)
    return jnp.concatenate([mean_g[:1], dev_g[:1]], axis=0)


def load_body(*refs):
    count = (len(refs) - 8) // 2
    sources, small, out_ref = refs[:count], refs[count : count + 6], refs[count + 6]
    targets, sem = refs[count + 7 : -1], refs[-1]
    copies = [
        pltpu.make_async_copy(source, target, sem.at[k])
        for k, (source, target) in enumerate(zip(sources, targets))
    ]
    for copy in copies:
        copy.start()
    prep_body(*small, out_ref)
    for copy in copies:
        copy.wait()


def prep_body(steps_ref, table_ref, scale_ref, embed_ref, gn_ref, ln_ref, out_ref):
    half = WIDTH // 2
    lane = lax.broadcasted_iota(jnp.int32, (1, WIDTH), 1)
    low = lane < half
    index = jnp.where(low, lane, lane - half).astype(F32)
    freqs = jnp.exp(index * (-math.log(10000.0) / half))
    table = table_ref[...]
    places = lax.broadcasted_iota(jnp.int32, table.shape, 0) * 128 + lax.broadcasted_iota(
        jnp.int32, table.shape, 1
    )
    pick = lambda t: jnp.sum(jnp.where(places == t, table, 0.0), keepdims=True)
    steps = [steps_ref[0:1, s : s + 1] for s in range(STEPS + 1)]
    levels = [pick(t) for t in steps]
    row = lambda value: jnp.broadcast_to(value, (1, WIDTH))
    rows = []
    for s in range(STEPS):
        angles = steps[s].astype(F32) * freqs
        wave = jnp.where(low, jnp.cos(angles), jnp.sin(angles))
        rows.append(scale_ref[...].reshape(1, WIDTH) * wave + embed_ref[...])
    rows = [r * jax.nn.sigmoid(r) for r in rows]
    for s in range(STEPS):
        now, after = levels[s], levels[s + 1]
        rows.append(row(jnp.sqrt(after / now)))
        rows.append(
            row(jnp.sqrt(1.0 - after) - jnp.sqrt(after) * jnp.sqrt(1.0 - now) / jnp.sqrt(now))
        )
    rows.append(gn_ref[...].reshape(1, WIDTH))
    rows.append(ln_ref[...].reshape(1, WIDTH))
    for r, value in enumerate(rows):
        out_ref[r : r + 1] = value


GN_ROW, LN_ROW = 3 * STEPS, 3 * STEPS + 1
EXTRA = 16
HEAD = COLS + EXTRA
PAD = 16
CHUNKS = 4


def stats_rows(stats):
    parts = []
    for _ in range(3):
        part = stats.astype(BF).astype(F32)
        parts.append(part)
        stats = stats - part
    rows = jnp.concatenate(parts + [jnp.zeros((EXTRA - 6, 128), F32)], axis=0)
    return jnp.concatenate([rows, jnp.zeros((EXTRA, WIDTH - 128), F32)], axis=1).astype(BF)


def stats_of(block_ref):
    rows = block_ref[COLS:HEAD, :128].astype(F32)
    return rows[0:2] + rows[2:4] + rows[4:6]


def merge(one, other):
    (count_a, mean_a, dev_a), (count_b, mean_b, dev_b) = one, other
    count, off = count_a + count_b, mean_b - mean_a
    scale = COLS * PER_GROUP * count_a * count_b / count
    return count, mean_a + off * (count_b / count), dev_a + dev_b + scale * (off * off)


def patches(count, stats):
    return count, stats[0:1], stats[1:2]


def first_body(x_ref, attn_ref, conv_ref, block_ref, state_ref, stats_ref, sem):
    places = ((attn_ref, 0), (conv_ref, HEAD))
    copies = [
        pltpu.make_async_copy(source, block_ref.at[pl.ds(start, COLS)], sem.at[k])
        for k, (source, start) in enumerate(places)
    ]
    for copy in copies:
        copy.start()
    x = x_ref[...]
    state_ref[...] = x
    stats = local_stats(x[0])
    stats_ref[0:2] = stats
    block_ref[COLS:HEAD] = stats_rows(stats)
    for copy in copies:
        copy.wait()


def pack_body(stats_ref, up_ref, down_ref, up_block_ref, down_block_ref):
    rows = stats_rows(stats_ref[0:2])
    for source, target in ((up_ref, up_block_ref), (down_ref, down_block_ref)):
        target[:COLS] = source[:COLS]
        target[COLS:] = rows


def partial_body(mine_ref, up_ref, down_ref, three_ref, two_ref):
    two = merge(patches(1, stats_of(up_ref)), patches(1, mine_ref[0:2]))
    three = merge(two, patches(1, stats_of(down_ref)))
    for (_, mean, dev), target in ((three, three_ref), (two, two_ref)):
        target[0:1], target[1:2] = mean, dev


def trim_body(rows, *refs):
    count = len(refs) // 2
    for source, target in zip(refs[:count], refs[count:]):
        target[...] = source[:rows]


def shifted(x):
    place = lax.broadcasted_iota(jnp.int32, x.shape, 0)
    before = jnp.where(place == 0, 0.0, pltpu.roll(x, 1, 0))
    after = jnp.where(place == COLS - 1, 0.0, pltpu.roll(x, COLS - 1, 0))
    return before, after


def conv_row(x, taps):
    before, after = shifted(x)
    return (
        dot(x.astype(BF), taps[1][...])
        + dot(before.astype(BF), taps[0][...])
        + dot(after.astype(BF), taps[2][...])
    )


def rims_body(start, place_ref, up_ref, down_ref, w_ref, out_ref):
    above = up_ref[start : start + COLS].astype(F32) * place_ref[0]
    below = down_ref[start : start + COLS].astype(F32) * place_ref[1]
    out_ref[...] = conv_row(above, [w_ref[0, t] for t in range(3)]) + conv_row(
        below, [w_ref[2, t] for t in range(3)]
    )


def level(step, moments, x, rims, prep_ref, taps, q_w):
    _, mean, dev = moments
    scale = 1.0 / jnp.sqrt(dev * (1.0 / (PATCHES * COLS * PER_GROUP)) + 1e-05)
    first_rows = lax.broadcasted_iota(jnp.int32, (8, 128), 0) < 4
    wide = dot_exact(jnp.where(first_rows, mean, scale), spread_matrix())
    x = x[0]
    normed = (x - wide[0:1]) * (wide[4:5] * prep_ref[GN_ROW : GN_ROW + 1])
    conv_in = normed * jax.nn.sigmoid(normed)
    hidden = x + (conv_row(conv_in, taps) + rims[...]) + prep_ref[step : step + 1]
    mid = jnp.mean(hidden, axis=1, keepdims=True)
    centered = hidden - mid
    var = jnp.mean(centered * centered, axis=1, keepdims=True)
    attn_in = (centered * (1.0 / jnp.sqrt(var + 1e-05)) * prep_ref[LN_ROW : LN_ROW + 1]).astype(BF)
    scale = (WIDTH // HEADS) ** (-0.5) * math.log2(math.e)
    query = (dot(attn_in, q_w[...]) * scale).astype(BF)
    return conv_in.astype(BF), hidden, attn_in, query


def level_body(x_ref, rims_ref, prep_ref, w_ref, q_ref, *refs):
    opposite_ref, conv_in_ref, h_ref, attn_in_ref, query_ref = refs[PATCHES - 1 :]
    total = patches(1, opposite_ref[0:2])
    for ref in refs[: PATCHES - 1]:
        total = merge(total, patches(1, stats_of(ref)))
    taps = [w_ref.at[1, t] for t in range(3)]
    conv_in_ref[:COLS], h_ref[...], attn_in_ref[...], query_ref[...] = level(
        0, total, x_ref[...], rims_ref, prep_ref, taps, q_ref
    )
    conv_in_ref[COLS:] = jnp.zeros((PAD, WIDTH), BF)


def keys_of(rows, kv_ref, out_ref):
    out_ref[...] = dot(jnp.concatenate([ref[:COLS] for ref in rows], axis=0), kv_ref[...]).astype(BF)


def keys_body(*refs):
    keys_of(refs[:-2], *refs[-2:])


def pair_scores(query_ref, parts, pair):
    first_half = lax.broadcasted_iota(jnp.int32, (COLS, 128), 1) < WIDTH // HEADS
    lanes = slice(pair * 128, (pair + 1) * 128)
    query = query_ref[:, lanes]
    zero = jnp.zeros_like(query)
    stacked = jnp.concatenate(
        [jnp.where(first_half, query, zero), jnp.where(first_half, zero, query)], axis=0
    )
    return [
        lax.dot_general(stacked, ref[:, lanes], (((1,), (1,)), ((), ())), preferred_element_type=F32)
        for ref in parts
    ]


def attend(query_ref, parts, mixed_ref):
    first_half = lax.broadcasted_iota(jnp.int32, (COLS, 128), 1) < WIDTH // HEADS
    following = pair_scores(query_ref, parts, 0)
    for pair in range(PAIRS):
        lanes = slice(pair * 128, (pair + 1) * 128)
        values = slice(WIDTH + pair * 128, WIDTH + (pair + 1) * 128)
        scores = following
        if pair + 1 < PAIRS:
            following = pair_scores(query_ref, parts, pair + 1)
        top = functools.reduce(jnp.maximum, [jnp.max(s, axis=1, keepdims=True) for s in scores])
        weights = [jnp.exp2(s - top) for s in scores]
        total = sum(jnp.sum(w, axis=1, keepdims=True) for w in weights)
        product = sum(dot(w.astype(BF), ref[:, values]) for w, ref in zip(weights, parts))
        product = product * (1.0 / total)
        mixed_ref[:, lanes] = jnp.where(first_half, product[:COLS], product[COLS:]).astype(BF)


def attend_body(early, late, ready, query_ref, h_ref, *refs):
    parts, rows, done = refs[:early], refs[early : early + 1 + late], refs[early + 1 + late :][:ready]
    kv_ref, out_w_ref, eps_ref, late_ref, mixed_ref = refs[early + 1 + late + ready :]
    keys_of(rows, kv_ref, late_ref.at[: (1 + late) * COLS])
    for ref in done:
        late_ref[COLS:] = ref[...]
    attend(query_ref, (*parts, late_ref), mixed_ref)
    eps_ref[...] = (h_ref[...] + dot(mixed_ref[...], out_w_ref[...])).astype(eps_ref.dtype)


def second_body(
    three_ref, before_ref, after_ref, x_ref, rims_ref, prep_ref, w_ref, q_ref, *refs
):
    attn_in_ref, h_ref, query_ref = refs
    total = merge(patches(3, three_ref[0:2]), patches(2, after_ref[0:2]))
    total = merge(total, patches(3, before_ref[0:2]))
    taps = [w_ref.at[1, t] for t in range(3)]
    _, h_ref[...], attn_in_ref[...], query_ref[...] = level(
        1, total, x_ref[...], rims_ref, prep_ref, taps, q_ref
    )


def guide(first, own, other):
    uncond = jnp.where(first, own, other)
    cond = jnp.where(first, other, own)
    return uncond + 3.0 * (cond - uncond)


def update_body(place_ref, prep_ref, x_ref, own_ref, other_ref, state_ref, stats_ref):
    own, other = own_ref[...].astype(F32), other_ref[...].astype(F32)
    guided = guide(place_ref[2] == 0.0, own, other)
    state = prep_ref[STEPS : STEPS + 1] * x_ref[0] + prep_ref[STEPS + 1 : STEPS + 2] * guided
    state_ref[0] = state
    stats_ref[0:2] = local_stats(state)


def last_body(
    place_ref, prep_ref, x_ref, own_ref, other_ref, state_ref, guided_ref, state_held, guided_held, sem
):
    row, step = STEPS + 2 * (STEPS - 1), COLS // CHUNKS
    copies = []
    for k in range(CHUNKS):
        part = slice(k * step, (k + 1) * step)
        own, other = own_ref[part].astype(F32), other_ref[part].astype(F32)
        guided = guide(place_ref[2] == 0.0, own, other)
        guided_held[part] = guided
        state_held[part] = prep_ref[row : row + 1] * x_ref[0, part] + prep_ref[row + 1 : row + 2] * guided
        for one, (held, target) in enumerate(((guided_held, guided_ref), (state_held, state_ref))):
            copy = pltpu.make_async_copy(held.at[part], target.at[0, part], sem.at[2 * k + one])
            copy.start()
            copies.append(copy)
    for copy in copies:
        copy.wait()


def shards(
    latent,
    stale_conv,
    stale_attn,
    cond_embed,
    timesteps,
    gn_gain,
    ln_gain,
    time_scale,
    conv_weight,
    q_weight,
    kv_weight,
    out_weight,
):
    patch, branch = lax.axis_index("patch"), lax.axis_index("cfg")
    place = jnp.stack([patch > 0, patch < PATCHES - 1, branch > 0]).astype(F32)
    upward = [(i, (i + 1) % PATCHES) for i in range(PATCHES)]
    downward = [(target, source) for source, target in upward]
    up = lambda x: lax.ppermute(x, "patch", upward)
    down = lambda x: lax.ppermute(x, "patch", downward)
    full = (COLS, WIDTH)
    whole = (1,) + full
    stats_shape = fast((8, 128), F32)
    shift = lambda x, far: lax.ppermute(
        x, "patch", [(i, (i + far) % PATCHES) for i in range(PATCHES)]
    )

    first, state, opposite = call(
        first_body,
        (fast((HEAD + COLS, WIDTH), BF), fast(whole, F32), fast((8, 128), F32)),
        (latent, HBM),
        (stale_attn.reshape(full), FAR),
        (stale_conv.reshape(full), FAR),
        scratch=(pltpu.SemaphoreType.DMA((2,)),),
        after=(place,),
    )
    table = np.ones((8, 128), np.float32)
    table.reshape(-1)[:1000] = alpha_table()
    weights = (conv_weight, q_weight, kv_weight, out_weight)
    trim = lambda rows, blocks, after=(): call(
        functools.partial(trim_body, rows),
        tuple(fast((rows, WIDTH), BF) for _ in blocks),
        *[(one, VMEM) for one in blocks],
        after=after,
    )

    ring1 = [up(first), down(first)]
    opposite = shift(opposite, PATCHES // 2)
    prep, conv_w, q_w, kv_w, out_w = call(
        load_body,
        (fast((8, WIDTH), F32),) + tuple(fast(w.shape, w.dtype) for w in weights),
        *[(w, FAR) for w in weights],
        (timesteps.reshape(1, -1), HBM),
        (jnp.asarray(table), HBM),
        (time_scale, HBM),
        (cond_embed, HBM),
        (gn_gain, HBM),
        (ln_gain, HBM),
        scratch=(pltpu.SemaphoreType.DMA((4,)),),
        after=(first,),
        limit=2,
    )
    passing = trim(HEAD, ring1, (prep, opposite))
    ring2 = [up(passing[0]), down(passing[1])]
    keys = lambda blocks, after=(): call(
        keys_body,
        fast((len(blocks) * COLS, 2 * WIDTH), BF),
        *[(one, VMEM) for one in blocks],
        (kv_w, VMEM),
        after=after,
    )
    conv_rims = lambda start, blocks, after=(): call(
        functools.partial(rims_body, start),
        fast(full, F32),
        (place, SCALARS),
        *[(one, VMEM) for one in blocks],
        (conv_w, VMEM),
        after=after,
    )
    rims = conv_rims(HEAD, ring1, (passing[0],))
    near_keys = keys(ring1, (rims,))
    ring2 = later(ring2, (near_keys,))
    ring3 = [up(ring2[0]), down(ring2[1])]
    mid_keys = keys(ring2, (ring2[0],))
    ring3 = later(ring3, (mid_keys,))
    ring4 = [up(ring3[0])]
    far_keys = keys(ring3, (ring3[0],))
    conv_in, hidden, attn_in, query = call(
        level_body,
        (fast((COLS + PAD, WIDTH), BF), fast(full, F32), fast(full, BF), fast(full, BF)),
        (state, VMEM),
        (rims, VMEM),
        (prep, VMEM),
        (conv_w, VMEM),
        (q_w, VMEM),
        *[(one, VMEM) for one in [first, *ring1, *ring2, *ring3, opposite]],
    )
    ring1 = [up(attn_in), down(attn_in)]
    attend_to = lambda weights, early, late, ready: call(
        functools.partial(attend_body, len(early), len(late), len(ready)),
        fast(full, BF),
        (query, VMEM),
        (hidden, VMEM),
        *early,
        (attn_in, VMEM),
        *[(one, VMEM) for one in late],
        *[(one, VMEM) for one in ready],
        *[(w, VMEM) for w in weights],
        scratch=(pltpu.VMEM((2 * COLS, 2 * WIDTH), BF), pltpu.VMEM(full, BF)),
        limit=20,
    )
    early = [(one, VMEM) for one in (near_keys, mid_keys, far_keys)]
    eps = attend_to((kv_w, out_w), early, ring4, [])
    exchange = lambda x: lax.ppermute(x, "cfg", [(0, 1), (1, 0)])
    other = exchange(eps)
    ring1 = later(ring1, (eps,))
    ring2 = [up(ring1[0]), down(ring1[1])]
    near_keys = keys(ring1, (eps,))
    (conv_in,) = later([conv_in], (near_keys,))
    rims_in = [up(conv_in), down(conv_in)]
    state, stats = call(
        update_body,
        (fast(whole, F32), stats_shape),
        (place, SCALARS),
        (prep, VMEM),
        (state, VMEM),
        (eps, VMEM),
        (other, VMEM),
        after=(near_keys,),
    )
    block = fast((HEAD, WIDTH), BF)
    packed = call(
        pack_body, (block, block), (stats, VMEM), *[(one, VMEM) for one in ring2], after=(state,)
    )
    ring3 = [up(packed[0]), down(packed[1])]
    rims = conv_rims(0, rims_in, (packed[0],))
    mid_keys = keys(ring2, (rims,))
    three, two = call(
        partial_body,
        (stats_shape, stats_shape),
        (stats, VMEM),
        *[(one, VMEM) for one in ring3],
        after=(mid_keys,),
    )
    before, behind = shift(three, 3), shift(two, -3)
    ring3 = later(ring3, (three,))
    ring4 = [up(ring3[0])]
    far_keys = keys(ring3, (ring3[0],))
    last_keys = keys(ring4, (far_keys,))
    attn_in, hidden, query = call(
        second_body,
        (fast(full, BF), fast(full, F32), fast(full, BF)),
        (three, VMEM),
        (before, VMEM),
        (behind, VMEM),
        (state, VMEM),
        (rims, VMEM),
        (prep, VMEM),
        (conv_w, VMEM),
        (q_w, VMEM),
        after=(last_keys,),
    )
    early = [(one, VMEM) for one in (near_keys, mid_keys, far_keys)]
    eps = attend_to((kv_w, out_w), early, [], [last_keys])
    other = exchange(eps)
    return call(
        last_body,
        (shape(whole, F32), shape(whole, F32)),
        (place, SCALARS),
        (prep, VMEM),
        (state, VMEM),
        (eps, VMEM),
        (other, VMEM),
        scratch=(
            pltpu.VMEM(full, F32),
            pltpu.VMEM(full, F32),
            pltpu.SemaphoreType.DMA((2 * CHUNKS,)),
        ),
        outs_far=True,
    )


def solution(mesh):
    placed = (
        P(("batch", "patch"), None, None),
        P("cfg", ("batch", "patch"), None, None),
        P("cfg", ("batch", "patch"), None, None),
        P(("batch", "cfg"), None),
        P(),
        P(),
        P(),
        P(),
        P(),
        P(),
        P(),
        P(),
    )
    return jax.shard_map(
        shards,
        mesh=mesh,
        in_specs=placed,
        out_specs=(P(("batch", "patch"), None, None), P(("batch", "patch"), None, None)),
        check_vma=False,
    )
```

```python
import functools
import math

import jax
import jax.numpy as jnp
import numpy as np
from jax import lax
from jax.experimental import pallas as pl
from jax.experimental.pallas import tpu as pltpu
from jax.sharding import PartitionSpec as P

HEADS = 10
GROUPS = 32
STEPS = 2
PATCHES = 8
COLS = 128
WIDTH = 640
PAIRS = HEADS // 2
PER_GROUP = WIDTH // GROUPS
BF = jnp.bfloat16
F32 = jnp.float32


def alpha_table():
    start, stop = np.float32(0.00085**0.5), np.float32(0.012**0.5)
    betas = np.linspace(start, stop, 1000, dtype=np.float32) ** 2
    return np.cumprod(1.0 - betas.astype(np.float64)).astype(np.float32)


def dot(a, b):
    return jnp.dot(a, b, preferred_element_type=F32)


def dot_exact(a, b):
    rows = a.shape[0]
    high = a.astype(BF).astype(F32)
    mid = (a - high).astype(BF).astype(F32)
    product = dot(jnp.concatenate([high, mid, (a - high) - mid], axis=0).astype(BF), b)
    return product[:rows] + (product[rows : 2 * rows] + product[2 * rows :])


HBM, FAR, VMEM, SCALARS = "hbm", "far", "vmem", "scalars"


class Arriving:
    def __init__(self, source, target, sem):
        self.copy = pltpu.make_async_copy(source, target, sem)
        self.target, self.waiting, self.shape = target, True, target.shape
        self.copy.start()

    def wait(self):
        if self.waiting:
            self.copy.wait()
            self.waiting = False

    def __getitem__(self, index):
        self.wait()
        return self.target[index]


def call(body, outs, *args, scratch=(), after=(), outs_far=False, limit=12):
    args += tuple((one, "token") for one in after)
    count, far = len(args), [i for i, (_, where) in enumerate(args) if where == HBM]
    leaves, tree = jax.tree.flatten(outs)
    specs = {
        HBM: pl.BlockSpec(memory_space=pl.ANY),
        FAR: pl.BlockSpec(memory_space=pl.ANY),
        "token": pl.BlockSpec(memory_space=pl.ANY),
        VMEM: pl.BlockSpec(memory_space=pltpu.VMEM),
        SCALARS: pl.BlockSpec(memory_space=pltpu.SMEM),
    }
    buffers = [pltpu.VMEM(args[i][0].shape, args[i][0].dtype) for i in far]
    if far:
        buffers.append(pltpu.SemaphoreType.DMA((len(far),)))

    def wrapped(*refs):
        ins, rest = list(refs[:count]), list(refs[count:])
        if far:
            held, sem = rest[-len(buffers) : -1], rest[-1]
            rest = rest[: -len(buffers)]
            for k, i in enumerate(far):
                ins[i] = Arriving(ins[i], held[k], sem.at[k])
        body(*ins[: count - len(after)], *rest)
        for i in far:
            ins[i].wait()

    def put(arg, where):
        if where not in (VMEM, HBM, FAR):
            return arg
        return pltpu.with_memory_space_constraint(arg, pltpu.VMEM if where == VMEM else pltpu.HBM)

    return pl.pallas_call(
        wrapped,
        out_shape=jax.tree.unflatten(tree, leaves),
        in_specs=[specs[where] for _, where in args],
        out_specs=jax.tree.unflatten(tree, [specs[FAR if outs_far else VMEM] for _ in leaves]),
        scratch_shapes=list(scratch) + buffers,
        compiler_params=pltpu.CompilerParams(vmem_limit_bytes=limit * 2**20),
    )(*[put(arg, where) for arg, where in args])


def fast(dims, dtype):
    return pltpu.VMEM(dims, dtype)


def later(arrays, after):
    count = len(arrays)
    spec = pl.BlockSpec(memory_space=pl.ANY)
    return list(pl.pallas_call(
        lambda *refs: None,
        out_shape=[shape(one.shape, one.dtype) for one in arrays],
        in_specs=[spec] * (count + len(after)),
        out_specs=[spec] * count,
        input_output_aliases={i: i for i in range(count)},
        cost_estimate=pl.CostEstimate(flops=0, bytes_accessed=0, transcendentals=0),
        compiler_params=pltpu.CompilerParams(vmem_limit_bytes=2**20),
    )(*arrays, *after))


def shape(dims, dtype):
    return jax.ShapeDtypeStruct(dims, dtype)


def group_matrix():
    channel = lax.broadcasted_iota(jnp.int32, (WIDTH, 128), 0)
    group = lax.broadcasted_iota(jnp.int32, (WIDTH, 128), 1)
    inside = (channel >= group * PER_GROUP) & (channel < (group + 1) * PER_GROUP)
    return jnp.where(inside, 1.0, 0.0).astype(BF)


def spread_matrix():
    group = lax.broadcasted_iota(jnp.int32, (128, WIDTH), 0)
    channel = lax.broadcasted_iota(jnp.int32, (128, WIDTH), 1)
    inside = (channel >= group * PER_GROUP) & (channel < (group + 1) * PER_GROUP)
    return jnp.where(inside, 1.0, 0.0).astype(BF)


def local_stats(x):
    gather, spread = group_matrix(), spread_matrix()
    mean_c = jnp.mean(x, axis=0, keepdims=True)
    centered = x - mean_c
    dev_c = jnp.sum(centered * centered, axis=0, keepdims=True)
    wide = lambda row: jnp.broadcast_to(row, (8, row.shape[1]))
    mean_g = dot_exact(wide(mean_c), gather) * (1.0 / PER_GROUP)
    off = wide(mean_c) - dot_exact(mean_g, spread)
    dev_g = dot_exact(wide(dev_c) + COLS * (off * off), gather)
    return jnp.concatenate([mean_g[:1], dev_g[:1]], axis=0)


def load_body(*refs):
    count = (len(refs) - 8) // 2
    sources, small, out_ref = refs[:count], refs[count : count + 6], refs[count + 6]
    targets, sem = refs[count + 7 : -1], refs[-1]
    copies = [
        pltpu.make_async_copy(source, target, sem.at[k])
        for k, (source, target) in enumerate(zip(sources, targets))
    ]
    for copy in copies:
        copy.start()
    prep_body(*small, out_ref)
    for copy in copies:
        copy.wait()


def prep_body(steps_ref, table_ref, scale_ref, embed_ref, gn_ref, ln_ref, out_ref):
    half = WIDTH // 2
    lane = lax.broadcasted_iota(jnp.int32, (1, WIDTH), 1)
    low = lane < half
    index = jnp.where(low, lane, lane - half).astype(F32)
    freqs = jnp.exp(index * (-math.log(10000.0) / half))
    table = table_ref[...]
    places = lax.broadcasted_iota(jnp.int32, table.shape, 0) * 128 + lax.broadcasted_iota(
        jnp.int32, table.shape, 1
    )
    pick = lambda t: jnp.sum(jnp.where(places == t, table, 0.0), keepdims=True)
    steps = [steps_ref[0:1, s : s + 1] for s in range(STEPS + 1)]
    levels = [pick(t) for t in steps]
    row = lambda value: jnp.broadcast_to(value, (1, WIDTH))
    rows = []
    for s in range(STEPS):
        angles = steps[s].astype(F32) * freqs
        wave = jnp.where(low, jnp.cos(angles), jnp.sin(angles))
        rows.append(scale_ref[...].reshape(1, WIDTH) * wave + embed_ref[...])
    rows = [r * jax.nn.sigmoid(r) for r in rows]
    for s in range(STEPS):
        now, after = levels[s], levels[s + 1]
        rows.append(row(jnp.sqrt(after / now)))
        rows.append(
            row(jnp.sqrt(1.0 - after) - jnp.sqrt(after) * jnp.sqrt(1.0 - now) / jnp.sqrt(now))
        )
    rows.append(gn_ref[...].reshape(1, WIDTH))
    rows.append(ln_ref[...].reshape(1, WIDTH))
    for r, value in enumerate(rows):
        out_ref[r : r + 1] = value


GN_ROW, LN_ROW = 3 * STEPS, 3 * STEPS + 1
EXTRA = 16
HEAD = COLS + EXTRA
PAD = 32
CHUNKS = 4


def stats_rows(stats):
    parts = []
    for _ in range(3):
        part = stats.astype(BF).astype(F32)
        parts.append(part)
        stats = stats - part
    rows = jnp.concatenate(parts + [jnp.zeros((EXTRA - 6, 128), F32)], axis=0)
    return jnp.concatenate([rows, jnp.zeros((EXTRA, WIDTH - 128), F32)], axis=1).astype(BF)


def stats_of(block_ref):
    rows = block_ref[COLS:HEAD, :128].astype(F32)
    return rows[0:2] + rows[2:4] + rows[4:6]


def merge(one, other):
    (count_a, mean_a, dev_a), (count_b, mean_b, dev_b) = one, other
    count, off = count_a + count_b, mean_b - mean_a
    scale = COLS * PER_GROUP * count_a * count_b / count
    return count, mean_a + off * (count_b / count), dev_a + dev_b + scale * (off * off)


def patches(count, stats):
    return count, stats[0:1], stats[1:2]


def first_body(x_ref, attn_ref, conv_ref, block_ref, state_ref, stats_ref, sem):
    places = ((attn_ref, 0), (conv_ref, HEAD))
    copies = [
        pltpu.make_async_copy(source, block_ref.at[pl.ds(start, COLS)], sem.at[k])
        for k, (source, start) in enumerate(places)
    ]
    for copy in copies:
        copy.start()
    x = x_ref[...]
    state_ref[...] = x
    stats = local_stats(x[0])
    stats_ref[0:2] = stats
    block_ref[COLS:HEAD] = stats_rows(stats)
    for copy in copies:
        copy.wait()


def pack_body(stats_ref, up_ref, down_ref, up_block_ref, down_block_ref):
    rows = stats_rows(stats_ref[0:2])
    for source, target in ((up_ref, up_block_ref), (down_ref, down_block_ref)):
        target[:COLS] = source[:COLS]
        target[COLS:] = rows


def partial_body(mine_ref, up_ref, down_ref, three_ref, two_ref):
    two = merge(patches(1, stats_of(up_ref)), patches(1, mine_ref[0:2]))
    three = merge(two, patches(1, stats_of(down_ref)))
    for (_, mean, dev), target in ((three, three_ref), (two, two_ref)):
        target[0:1], target[1:2] = mean, dev


def trim_body(rows, *refs):
    count = len(refs) // 2
    for source, target in zip(refs[:count], refs[count:]):
        target[...] = source[:rows]


def shifted(x):
    place = lax.broadcasted_iota(jnp.int32, x.shape, 0)
    before = jnp.where(place == 0, 0.0, pltpu.roll(x, 1, 0))
    after = jnp.where(place == COLS - 1, 0.0, pltpu.roll(x, COLS - 1, 0))
    return before, after


def conv_row(x, taps):
    before, after = shifted(x)
    return (
        dot(x.astype(BF), taps[1][...])
        + dot(before.astype(BF), taps[0][...])
        + dot(after.astype(BF), taps[2][...])
    )


def rims_body(start, place_ref, up_ref, down_ref, w_ref, out_ref):
    above = up_ref[start : start + COLS].astype(F32) * place_ref[0]
    below = down_ref[start : start + COLS].astype(F32) * place_ref[1]
    out_ref[...] = conv_row(above, [w_ref[0, t] for t in range(3)]) + conv_row(
        below, [w_ref[2, t] for t in range(3)]
    )


def level(step, moments, x, rims, prep_ref, taps, q_w):
    _, mean, dev = moments
    scale = 1.0 / jnp.sqrt(dev * (1.0 / (PATCHES * COLS * PER_GROUP)) + 1e-05)
    first_rows = lax.broadcasted_iota(jnp.int32, (8, 128), 0) < 4
    wide = dot_exact(jnp.where(first_rows, mean, scale), spread_matrix())
    x = x[0]
    normed = (x - wide[0:1]) * (wide[4:5] * prep_ref[GN_ROW : GN_ROW + 1])
    conv_in = normed * jax.nn.sigmoid(normed)
    hidden = x + (conv_row(conv_in, taps) + rims[...]) + prep_ref[step : step + 1]
    mid = jnp.mean(hidden, axis=1, keepdims=True)
    centered = hidden - mid
    var = jnp.mean(centered * centered, axis=1, keepdims=True)
    attn_in = (centered * (1.0 / jnp.sqrt(var + 1e-05)) * prep_ref[LN_ROW : LN_ROW + 1]).astype(BF)
    scale = (WIDTH // HEADS) ** (-0.5) * math.log2(math.e)
    query = (dot(attn_in, q_w[...]) * scale).astype(BF)
    return conv_in.astype(BF), hidden, attn_in, query


def level_body(x_ref, rims_ref, prep_ref, w_ref, q_ref, *refs):
    opposite_ref, conv_in_ref, h_ref, attn_in_ref, query_ref = refs[PATCHES - 1 :]
    total = patches(1, opposite_ref[0:2])
    for ref in refs[: PATCHES - 1]:
        total = merge(total, patches(1, stats_of(ref)))
    taps = [w_ref.at[1, t] for t in range(3)]
    conv_in_ref[:COLS], h_ref[...], attn_in_ref[...], query_ref[...] = level(
        0, total, x_ref[...], rims_ref, prep_ref, taps, q_ref
    )
    conv_in_ref[COLS:] = jnp.zeros((PAD, WIDTH), BF)


def keys_of(rows, kv_ref, out_ref):
    out_ref[...] = dot(jnp.concatenate([ref[:COLS] for ref in rows], axis=0), kv_ref[...]).astype(BF)


def keys_body(*refs):
    keys_of(refs[:-2], *refs[-2:])


def pair_scores(query_ref, parts, pair):
    first_half = lax.broadcasted_iota(jnp.int32, (COLS, 128), 1) < WIDTH // HEADS
    lanes = slice(pair * 128, (pair + 1) * 128)
    query = query_ref[:, lanes]
    zero = jnp.zeros_like(query)
    stacked = jnp.concatenate(
        [jnp.where(first_half, query, zero), jnp.where(first_half, zero, query)], axis=0
    )
    return [
        lax.dot_general(stacked, ref[:, lanes], (((1,), (1,)), ((), ())), preferred_element_type=F32)
        for ref in parts
    ]


def attend(query_ref, parts, mixed_ref):
    first_half = lax.broadcasted_iota(jnp.int32, (COLS, 128), 1) < WIDTH // HEADS
    following = pair_scores(query_ref, parts, 0)
    for pair in range(PAIRS):
        lanes = slice(pair * 128, (pair + 1) * 128)
        values = slice(WIDTH + pair * 128, WIDTH + (pair + 1) * 128)
        scores = following
        if pair + 1 < PAIRS:
            following = pair_scores(query_ref, parts, pair + 1)
        top = functools.reduce(jnp.maximum, [jnp.max(s, axis=1, keepdims=True) for s in scores])
        weights = [jnp.exp2(s - top) for s in scores]
        total = sum(jnp.sum(w, axis=1, keepdims=True) for w in weights)
        product = sum(dot(w.astype(BF), ref[:, values]) for w, ref in zip(weights, parts))
        product = product * (1.0 / total)
        mixed_ref[:, lanes] = jnp.where(first_half, product[:COLS], product[COLS:]).astype(BF)


def attend_body(early, late, ready, query_ref, h_ref, *refs):
    parts, rows, done = refs[:early], refs[early : early + 1 + late], refs[early + 1 + late :][:ready]
    kv_ref, out_w_ref, eps_ref, late_ref, mixed_ref = refs[early + 1 + late + ready :]
    keys_of(rows, kv_ref, late_ref.at[: (1 + late) * COLS])
    for ref in done:
        late_ref[COLS:] = ref[...]
    attend(query_ref, (*parts, late_ref), mixed_ref)
    eps_ref[...] = (h_ref[...] + dot(mixed_ref[...], out_w_ref[...])).astype(eps_ref.dtype)


def second_body(
    three_ref, before_ref, after_ref, x_ref, rims_ref, prep_ref, w_ref, q_ref, *refs
):
    attn_in_ref, h_ref, query_ref = refs
    total = merge(patches(3, three_ref[0:2]), patches(2, after_ref[0:2]))
    total = merge(total, patches(3, before_ref[0:2]))
    taps = [w_ref.at[1, t] for t in range(3)]
    _, h_ref[...], attn_in_ref[...], query_ref[...] = level(
        1, total, x_ref[...], rims_ref, prep_ref, taps, q_ref
    )


def guide(first, own, other):
    uncond = jnp.where(first, own, other)
    cond = jnp.where(first, other, own)
    return uncond + 3.0 * (cond - uncond)


def update_body(place_ref, prep_ref, x_ref, own_ref, other_ref, state_ref, stats_ref):
    own, other = own_ref[...].astype(F32), other_ref[...].astype(F32)
    guided = guide(place_ref[2] == 0.0, own, other)
    state = prep_ref[STEPS : STEPS + 1] * x_ref[0] + prep_ref[STEPS + 1 : STEPS + 2] * guided
    state_ref[0] = state
    stats_ref[0:2] = local_stats(state)


def last_body(
    place_ref, prep_ref, x_ref, own_ref, other_ref, state_ref, guided_ref, state_held, guided_held, sem
):
    row, step = STEPS + 2 * (STEPS - 1), COLS // CHUNKS
    copies = []
    for k in range(CHUNKS):
        part = slice(k * step, (k + 1) * step)
        own, other = own_ref[part].astype(F32), other_ref[part].astype(F32)
        guided = guide(place_ref[2] == 0.0, own, other)
        guided_held[part] = guided
        state_held[part] = prep_ref[row : row + 1] * x_ref[0, part] + prep_ref[row + 1 : row + 2] * guided
        for one, (held, target) in enumerate(((guided_held, guided_ref), (state_held, state_ref))):
            copy = pltpu.make_async_copy(held.at[part], target.at[0, part], sem.at[2 * k + one])
            copy.start()
            copies.append(copy)
    for copy in copies:
        copy.wait()


def shards(
    latent,
    stale_conv,
    stale_attn,
    cond_embed,
    timesteps,
    gn_gain,
    ln_gain,
    time_scale,
    conv_weight,
    q_weight,
    kv_weight,
    out_weight,
):
    patch, branch = lax.axis_index("patch"), lax.axis_index("cfg")
    place = jnp.stack([patch > 0, patch < PATCHES - 1, branch > 0]).astype(F32)
    upward = [(i, (i + 1) % PATCHES) for i in range(PATCHES)]
    downward = [(target, source) for source, target in upward]
    up = lambda x: lax.ppermute(x, "patch", upward)
    down = lambda x: lax.ppermute(x, "patch", downward)
    full = (COLS, WIDTH)
    whole = (1,) + full
    stats_shape = fast((8, 128), F32)
    shift = lambda x, far: lax.ppermute(
        x, "patch", [(i, (i + far) % PATCHES) for i in range(PATCHES)]
    )

    first, state, opposite = call(
        first_body,
        (fast((HEAD + COLS, WIDTH), BF), fast(whole, F32), fast((8, 128), F32)),
        (latent, HBM),
        (stale_attn.reshape(full), FAR),
        (stale_conv.reshape(full), FAR),
        scratch=(pltpu.SemaphoreType.DMA((2,)),),
        after=(place,),
    )
    table = np.ones((8, 128), np.float32)
    table.reshape(-1)[:1000] = alpha_table()
    weights = (conv_weight, q_weight, kv_weight, out_weight)
    trim = lambda rows, blocks, after=(): call(
        functools.partial(trim_body, rows),
        tuple(fast((rows, WIDTH), BF) for _ in blocks),
        *[(one, VMEM) for one in blocks],
        after=after,
    )

    ring1 = [up(first), down(first)]
    opposite = shift(opposite, PATCHES // 2)
    prep, conv_w, q_w, kv_w, out_w = call(
        load_body,
        (fast((8, WIDTH), F32),) + tuple(fast(w.shape, w.dtype) for w in weights),
        *[(w, FAR) for w in weights],
        (timesteps.reshape(1, -1), HBM),
        (jnp.asarray(table), HBM),
        (time_scale, HBM),
        (cond_embed, HBM),
        (gn_gain, HBM),
        (ln_gain, HBM),
        scratch=(pltpu.SemaphoreType.DMA((4,)),),
        after=(first,),
        limit=2,
    )
    passing = [*trim(HEAD, ring1[:1], (prep,)), *trim(HEAD, ring1[1:], (prep, opposite))]
    ring2 = [up(passing[0]), down(passing[1])]
    keys = lambda blocks, after=(): call(
        keys_body,
        fast((len(blocks) * COLS, 2 * WIDTH), BF),
        *[(one, VMEM) for one in blocks],
        (kv_w, VMEM),
        after=after,
    )
    conv_rims = lambda start, blocks, after=(): call(
        functools.partial(rims_body, start),
        fast(full, F32),
        (place, SCALARS),
        *[(one, VMEM) for one in blocks],
        (conv_w, VMEM),
        after=after,
    )
    rims = conv_rims(HEAD, ring1, (passing[0],))
    near_keys = keys(ring1, (rims,))
    ring2 = later(ring2, (near_keys,))
    ring3 = [up(ring2[0]), down(ring2[1])]
    mid_keys = keys(ring2, (ring2[0],))
    ring3 = later(ring3, (mid_keys,))
    ring4 = [up(ring3[0])]
    far_keys = keys(ring3, (ring3[0],))
    conv_in, hidden, attn_in, query = call(
        level_body,
        (fast((COLS + PAD, WIDTH), BF), fast(full, F32), fast(full, BF), fast(full, BF)),
        (state, VMEM),
        (rims, VMEM),
        (prep, VMEM),
        (conv_w, VMEM),
        (q_w, VMEM),
        *[(one, VMEM) for one in [first, *ring1, *ring2, *ring3, opposite]],
    )
    ring1 = [up(attn_in), down(attn_in)]
    attend_to = lambda weights, early, late, ready: call(
        functools.partial(attend_body, len(early), len(late), len(ready)),
        fast(full, BF),
        (query, VMEM),
        (hidden, VMEM),
        *early,
        (attn_in, VMEM),
        *[(one, VMEM) for one in late],
        *[(one, VMEM) for one in ready],
        *[(w, VMEM) for w in weights],
        scratch=(pltpu.VMEM((2 * COLS, 2 * WIDTH), BF), pltpu.VMEM(full, BF)),
        limit=20,
    )
    early = [(one, VMEM) for one in (near_keys, mid_keys, far_keys)]
    eps = attend_to((kv_w, out_w), early, ring4, [])
    exchange = lambda x: lax.ppermute(x, "cfg", [(0, 1), (1, 0)])
    other = exchange(eps)
    ring1 = later(ring1, (eps,))
    ring2 = [up(ring1[0]), down(ring1[1])]
    near_keys = keys(ring1, (eps,))
    (conv_in,) = later([conv_in], (near_keys,))
    rims_in = [up(conv_in), down(conv_in)]
    state, stats = call(
        update_body,
        (fast(whole, F32), stats_shape),
        (place, SCALARS),
        (prep, VMEM),
        (state, VMEM),
        (eps, VMEM),
        (other, VMEM),
        after=(near_keys,),
    )
    block = fast((HEAD, WIDTH), BF)
    packed = call(
        pack_body, (block, block), (stats, VMEM), *[(one, VMEM) for one in ring2], after=(state,)
    )
    ring3 = [up(packed[0]), down(packed[1])]
    rims = conv_rims(0, rims_in, (packed[0],))
    mid_keys = keys(ring2, (rims,))
    three, two = call(
        partial_body,
        (stats_shape, stats_shape),
        (stats, VMEM),
        *[(one, VMEM) for one in ring3],
        after=(mid_keys,),
    )
    before, behind = shift(three, 3), shift(two, -3)
    ring3 = later(ring3, (three,))
    ring4 = [up(ring3[0])]
    far_keys = keys(ring3, (ring3[0],))
    last_keys = keys(ring4, (far_keys,))
    attn_in, hidden, query = call(
        second_body,
        (fast(full, BF), fast(full, F32), fast(full, BF)),
        (three, VMEM),
        (before, VMEM),
        (behind, VMEM),
        (state, VMEM),
        (rims, VMEM),
        (prep, VMEM),
        (conv_w, VMEM),
        (q_w, VMEM),
        after=(last_keys,),
    )
    early = [(one, VMEM) for one in (near_keys, mid_keys, far_keys)]
    eps = attend_to((kv_w, out_w), early, [], [last_keys])
    other = exchange(eps)
    return call(
        last_body,
        (shape(whole, F32), shape(whole, F32)),
        (place, SCALARS),
        (prep, VMEM),
        (state, VMEM),
        (eps, VMEM),
        (other, VMEM),
        scratch=(
            pltpu.VMEM(full, F32),
            pltpu.VMEM(full, F32),
            pltpu.SemaphoreType.DMA((2 * CHUNKS,)),
        ),
        outs_far=True,
    )


def solution(mesh):
    placed = (
        P(("batch", "patch"), None, None),
        P("cfg", ("batch", "patch"), None, None),
        P("cfg", ("batch", "patch"), None, None),
        P(("batch", "cfg"), None),
        P(),
        P(),
        P(),
        P(),
        P(),
        P(),
        P(),
        P(),
    )
    return jax.shard_map(
        shards,
        mesh=mesh,
        in_specs=placed,
        out_specs=(P(("batch", "patch"), None, None), P(("batch", "patch"), None, None)),
        check_vma=False,
    )
```
